512 devices in a mesh: pipe: 8 (over x, core), expert: 64 (over y, z).
Axes of the slice: x: 4, y: 8, z: 8, core: 2. Of those that a mesh axis runs over, the one named last changes fastest.
Arguments:
- act_down: bfloat16 [8, 4096, 3584], P('pipe', 'expert'), may hold values from -6 to 6
- act_up: bfloat16 [8, 4096, 3584], P('pipe', 'expert'), may hold values from -6 to 6
- norm_gain: bfloat16 [8, 3584], P('pipe'), may hold values from 0.5 to 1.5
- gate_weight: bfloat16 [8, 8192, 3584], P('pipe', 'expert'), may hold values from -0.09375 to 0.09375
- up_weight: bfloat16 [8, 8192, 3584], P('pipe', 'expert'), may hold values from -0.09375 to 0.09375
- down_weight: bfloat16 [8, 1024, 28672], P('pipe', None, 'expert'), may hold values from -0.1875 to 0.1875
- routes_down: int32 [8, 4096, 1], P('pipe', 'expert'), may hold values from 0 to 7; in each aligned block of 64 rows (0 to 63, 64 to 127, ..., all dimensions but the last counted through in order) at most 10 rows name the same one
- gates_down: float32 [8, 4096, 1], P('pipe', 'expert'), may hold values from 0.5 to 2
- routes_up: int32 [8, 4096, 1], P('pipe', 'expert'), may hold values from 0 to 7; in each aligned block of 64 rows (0 to 63, 64 to 127, ..., all dimensions but the last counted through in order) at most 10 rows name the same one
- gates_up: float32 [8, 4096, 1], P('pipe', 'expert'), may hold values from 0.5 to 2
Outputs:
- out_down: bfloat16 [8, 4096, 3584], P('pipe', 'expert')
- out_up: bfloat16 [8, 4096, 3584], P('pipe', 'expert')
The draws below stay inside these ranges and needn't reach their ends.
Inputs may be any that keep to these rules, and one draw needn't show every extreme that they name: `routes_down`: the 1 expert named by one token are all different. In the rows of one device (aligned blocks of 64 rows), no expert is named by more than 10 rows, a bound that some block reaches. `routes_up`: as for routes_down.
All inputs are finite; a program needn't handle non-finite values.
Results may differ from the reference program's by a relative error of at most 0.0055.
Values may be sent and summed in bfloat16 or wider, within the bound.
A program may use at most 128 MiB of HBM per device.

```python
import math
import jax
import jax.numpy as jnp
import numpy as np
from jax import lax

D = 3584
FF = 1024
EXPERTS = 8
TOP = 1
TOK_DEV = 64
CAP = 10
TOKENS = 4096
N_PIPE = 8


def levels(key, shape, pieces, least, largest):
    def one(position, blocks):
        draws = jax.random.uniform(jax.random.fold_in(jax.random.fold_in(key, 6), position), (blocks,), jnp.float32, least / len(pieces), largest / len(pieces))
        return jnp.repeat(jnp.exp(draws), shape[position] // blocks).reshape((-1,) + (1,) * (len(shape) - position - 1))

    factor_of = one(*pieces[0])
    for cut in pieces[1:]:
        factor_of = factor_of * one(*cut)
    return factor_of


def assign_block(rng, own, number, rows, number_of, top, most, skew):
    order = jax.random.permutation(rng, number_of)
    heavy_load, ordinary = shares(number_of, rows * top, most, skew, True), shares(number_of, rows * top, most, skew, False)
    places = jnp.arange(number_of)

    def named(sizes, offset_by):
        used = int((sizes > 0).sum())
        fixed = max(1, used // 4)
        moved = fixed + (places - fixed + offset_by * (used - fixed)) % max(1, number_of - fixed)
        return jnp.zeros((number_of,), jnp.int32).at[order[jnp.where(places < fixed, places, moved)]].set(jnp.asarray(sizes, jnp.int32))

    sizes = jnp.where(number % 4 == 0, named(heavy_load, number // 4), named(ordinary, number - number // 4 - 1))
    mixed = jax.random.permutation(jax.random.fold_in(own, 3), number_of)
    donor, sink = mixed[0:number_of // 2 * 2:2], mixed[1:number_of // 2 * 2:2]
    margin = jnp.minimum(sizes[donor] - 1, most - sizes[sink]) // 2
    margin = jnp.where((donor == order[0]) | (sink == order[0]) | (sizes[sink] == 0), 0, jnp.maximum(margin, 0))
    moved = jax.random.randint(jax.random.fold_in(own, 4), (number_of // 2,), 0, 1 << 20) % (margin + 1)
    sizes = sizes.at[donor].add(-moved).at[sink].add(moved)
    members = jnp.searchsorted(jnp.cumsum(sizes), jnp.arange(rows * top), side="right").astype(jnp.int32)
    table = members.reshape(top, rows).T
    table = table[jax.random.permutation(jax.random.fold_in(own, 1), rows)]
    offset_by = jax.random.randint(jax.random.fold_in(own, 2), (rows, 1), 0, top)
    return jnp.take_along_axis(table, (jnp.arange(top)[None, :] + offset_by) % top, axis=1)


def shares(count, total, bound, slope, full):
    loads = [(1 << 20) // math.isqrt(rank ** slope) + 1 for rank in range(1, count + 1)]
    largest = bound if full else min(bound, max(-(-total // count), total * loads[0] // sum(loads)))
    least = 1 if total - largest >= count - 1 else 0
    holding, rest = [largest] + [least] * (count - 1), total - largest - least * (count - 1)
    while rest > 0:
        free = [i for i in range(1, count) if holding[i] < largest] or [i for i in range(1, count) if holding[i] < bound]
        whole, budget = sum([loads[i] for i in free]), rest
        for i in free:
            extra = min(bound - holding[i], max(1, budget * loads[i] // whole), rest)
            holding[i] = holding[i] + extra
            rest = rest - extra
    return np.array(holding)


def normal_values(stream_key, extent, width, limit, split=(), kind=jnp.bfloat16):
    level = levels(stream_key, extent, split, -0.22, 0.18) if split else 1.0
    result = jax.random.normal(stream_key, extent, jnp.float32) * width * level
    return jnp.minimum(jnp.maximum(result, -limit), limit).astype(kind)


def setup_inputs(seed: int = 0) -> dict:
    seeds = jax.random.split(jax.random.key(seed), 11)
    act_down = normal_values(seeds[0], (N_PIPE, TOKENS, D), 1.0, 6.0, ((0, 8), (1, 64)))
    act_up = normal_values(seeds[1], (N_PIPE, TOKENS, D), 1.0, 6.0, ((0, 8), (1, 64)))
    norm_gain = jnp.clip(1.0 + 0.1 * jax.random.normal(seeds[2], (N_PIPE, D), jnp.float32), 0.5, 1.5).astype(jnp.bfloat16)
    gate_weight = normal_values(seeds[3], (N_PIPE, EXPERTS * FF, D), D ** -0.5, 0.09375, ((0, 8), (1, 64)))
    up_weight = normal_values(seeds[4], (N_PIPE, EXPERTS * FF, D), D ** -0.5, 0.09375, ((0, 8), (1, 64)))
    down_weight = normal_values(seeds[5], (N_PIPE, FF, EXPERTS * D), FF ** -0.5, 0.1875, ((0, 8), (2, 64)))
    routes_down_keys = jax.random.split(jax.random.fold_in(seeds[6], 1), N_PIPE * TOKENS // TOK_DEV)
    routes_down_turns = jax.random.permutation(jax.random.fold_in(seeds[6], 3), N_PIPE * TOKENS // TOK_DEV)
    routes_down = jax.vmap(lambda own, number: assign_block(jax.random.fold_in(seeds[6], 2), own, number, TOK_DEV, EXPERTS, TOP, CAP, 2))(routes_down_keys, routes_down_turns).reshape((N_PIPE, TOKENS, TOP))
    gates_down = jnp.clip(0.5 + 1.5 * jax.random.uniform(seeds[7], (N_PIPE, TOKENS, TOP), jnp.float32) ** levels(seeds[7], (N_PIPE, TOKENS, TOP), ((0, 8), (1, 64)), -0.2, 0.2), 0.5, 2.0)
    routes_up_keys = jax.random.split(jax.random.fold_in(seeds[8], 1), N_PIPE * TOKENS // TOK_DEV)
    routes_up_turns = jax.random.permutation(jax.random.fold_in(seeds[8], 3), N_PIPE * TOKENS // TOK_DEV)
    routes_up = jax.vmap(lambda own, number: assign_block(jax.random.fold_in(seeds[8], 2), own, number, TOK_DEV, EXPERTS, TOP, CAP, 2))(routes_up_keys, routes_up_turns).reshape((N_PIPE, TOKENS, TOP))
    gates_up = jnp.clip(0.5 + 1.5 * jax.random.uniform(seeds[9], (N_PIPE, TOKENS, TOP), jnp.float32) ** levels(seeds[9], (N_PIPE, TOKENS, TOP), ((0, 8), (1, 64)), -0.2, 0.2), 0.5, 2.0)
    return {"act_down": act_down, "act_up": act_up, "norm_gain": norm_gain, "gate_weight": gate_weight, "up_weight": up_weight, "down_weight": down_weight, "routes_down": routes_down, "gates_down": gates_down, "routes_up": routes_up, "gates_up": gates_up}


EPSILON = 1e-06

def apply_layer(activations, norm_scale, routes, gate_weights, gate_rows, up_rows, down_cols):
    widened = activations.astype(jnp.float32)
    inverse_rms = lax.rsqrt(lax.optimization_barrier(jnp.mean(widened * widened, axis=-1, keepdims=True)) + EPSILON)
    normed = (widened * inverse_rms * norm_scale.astype(jnp.float32)).astype(jnp.bfloat16)
    choosers = (routes[:, :, None] == jnp.arange(EXPERTS, dtype=jnp.int32)[None, None, :]).astype(jnp.float32)
    mixing = lax.optimization_barrier(jnp.sum(choosers * gate_weights[:, :, None], axis=1))
    total = widened
    for expert in range(EXPERTS):
        gate_part = gate_rows[expert * FF:(expert + 1) * FF]
        up_part = up_rows[expert * FF:(expert + 1) * FF]
        down_part = down_cols[:, expert * D:(expert + 1) * D]
        gate_pre = jnp.dot(normed, gate_part.T, preferred_element_type=jnp.float32)
        up_pre = jnp.dot(normed, up_part.T, preferred_element_type=jnp.float32)
        activated = (jax.nn.silu(gate_pre) * up_pre).astype(jnp.bfloat16)
        expert_raw = jnp.dot(activated, down_part, preferred_element_type=jnp.float32)
        expert_out = lax.optimization_barrier(expert_raw.astype(jnp.bfloat16)).astype(jnp.float32)
        total = total + mixing[:, expert:expert + 1] * expert_out
    return total.astype(jnp.bfloat16)

def reference(act_down, act_up, norm_gain, gate_weight, up_weight, down_weight, routes_down, gates_down, routes_up, gates_up):
    first_down = []
    first_up = []
    for section in range(N_PIPE):
        first_down.append(apply_layer(act_down[section], norm_gain[section], routes_down[section], gates_down[section], gate_weight[section], up_weight[section], down_weight[section]))
        first_up.append(apply_layer(act_up[section], norm_gain[section], routes_up[section], gates_up[section], gate_weight[section], up_weight[section], down_weight[section]))
    out_down = jnp.stack([first_up[0]] + first_down[:-1])
    out_up = jnp.stack(first_up[1:] + [first_down[-1]])
    return (out_down, out_up)
```

```python
import functools

import jax
import jax.numpy as jnp
from jax import lax
from jax.experimental import pallas as pl
from jax.experimental.pallas import tpu as pltpu
from jax.sharding import PartitionSpec as P

EXPERTS = 8
CAP = 10
SLAB = 16
CHUNKS = 4
EPSILON = 1e-06

MESH = pl.DeviceIdType.MESH
F32 = jnp.float32
BF16 = jnp.bfloat16


def one_hot(condition):
    return jnp.where(condition, 1.0, 0.0).astype(BF16)


def iota(shape, dimension):
    return lax.broadcasted_iota(jnp.int32, shape, dimension)


def kernel(
    experts,
    sections,
    x_down,
    x_up,
    gain,
    gate_w,
    up_w,
    down_w,
    route_rows,
    route_cols_down,
    route_cols_up,
    gate_cols_down,
    gate_cols_up,
    out_down,
    out_up,
    gate_up,
    normed,
    slabs,
    landed,
    tokens,
    hidden_own,
    hidden,
    columns,
    returned,
    spread,
    final,
    residual,
    mixing,
    mixing_here,
    slab_send,
    slab_recv,
    token_send,
    token_recv,
    hidden_send,
    hidden_recv,
    hidden_copy,
    columns_send,
    columns_recv,
    final_send,
    final_send_same,
    final_recv,
    residual_send,
    residual_recv,
    mixing_send,
    mixing_recv,
):
    ring = tokens.shape[2]
    rows = experts * CAP
    slots = experts * SLAB
    count, depth = x_down.shape
    width = depth // CHUNKS
    units = gate_w.shape[0]
    pipe = lax.axis_index("pipe")
    position = lax.axis_index("expert")
    y = position // ring
    z = position % ring
    x_refs = (x_down, x_up)
    route_cols = (route_cols_down, route_cols_up)
    gate_cols = (gate_cols_down, gate_cols_up)
    outs = (out_down, out_up)

    def at_y(k):
        return (pipe, lax.rem(y + k, experts) * ring + z)

    def at_z(k):
        return (pipe, y * ring + lax.rem(z + k, ring))

    barrier = pltpu.get_barrier_semaphore()

    def greet(device):
        pl.semaphore_signal(barrier, inc=1, device_id=device, device_id_type=MESH)

    @pl.loop(1, experts)
    def _(k):
        greet(at_y(k))

    @pl.loop(1, ring)
    def _(k):
        greet(at_z(k))

    @pl.when(pipe > 0)
    def _():
        @pl.loop(0, experts)
        def _(k):
            greet((pipe - 1, k * ring + z))

    @pl.when(pipe < sections - 1)
    def _():
        @pl.loop(0, experts)
        def _(k):
            greet((pipe + 1, k * ring + z))

    neighbours = jnp.where(pipe > 0, 1, 0) + jnp.where(pipe < sections - 1, 1, 0)
    greeted = experts - 1 + ring - 1 + experts * neighbours

    def wait(ref, sem):
        pltpu.make_async_copy(ref, ref, sem).wait()

    def normalize(g):
        x_ref = x_refs[g]
        total = jnp.zeros((count, 1), F32)
        for c in range(CHUNKS):
            part = x_ref[:, c * width : (c + 1) * width].astype(F32)
            total = total + jnp.sum(part * part, axis=-1, keepdims=True)
        inverse = lax.rsqrt(total / depth + EPSILON)
        for c in range(CHUNKS):
            cut = slice(c * width, (c + 1) * width)
            part = x_ref[:, cut].astype(F32)
            normed[g, :, cut] = (part * inverse * gain[:, cut].astype(F32)).astype(BF16)

    def pick(g):
        slot = iota((slots, count), 0)
        named = one_hot(route_rows[g : g + 1, :] == slot // SLAB)
        earlier = one_hot(iota((count, count), 0) < iota((count, count), 1))
        rank = jnp.dot(named, earlier, preferred_element_type=F32)
        same = rank == (slot % SLAB).astype(F32)
        return jnp.where(same, named.astype(F32), 0.0).astype(BF16)

    def mix(g):
        slot = iota((count, slots), 1)
        named = one_hot(route_cols[g][...] == slot // SLAB)
        earlier = one_hot(iota((count, count), 1) < iota((count, count), 0))
        rank = jnp.dot(earlier, named, preferred_element_type=F32)
        same = rank == (slot % SLAB).astype(F32)
        mixing[g] = jnp.where(same, named.astype(F32), 0.0) * gate_cols[g][...]

    def slab(k):
        return pl.ds(pl.multiple_of(k * SLAB, SLAB), SLAB)

    def dispatch(g, c, picker):
        cut = slice(c * width, (c + 1) * width)
        slabs[g, c] = jnp.dot(
            picker, normed[g, :, cut], preferred_element_type=F32
        ).astype(BF16)
        pltpu.make_async_copy(
            slabs.at[g, c, slab(y)], landed.at[g, c, slab(y)], slab_recv.at[g, c]
        ).start()

        @pl.loop(1, experts)
        def _(k):
            pltpu.make_async_remote_copy(
                src_ref=slabs.at[g, c, slab(lax.rem(y + k, experts))],
                dst_ref=landed.at[g, c, slab(y)],
                send_sem=slab_send.at[g, c],
                recv_sem=slab_recv.at[g, c],
                device_id=at_y(k),
                device_id_type=MESH,
            ).start()

    def last(g):
        return pipe == (sections - 1 if g == 0 else 0)

    def onward(g):
        return pipe + 1 if g == 0 else pipe - 1

    def send_residual(g):
        pairs = (
            (x_refs[g], residual, residual_send, residual_recv),
            (mixing.at[g], mixing_here, mixing_send, mixing_recv),
        )

        @pl.when(last(g))
        def _():
            for source, target, _, sem in pairs:
                pltpu.make_async_copy(source, target.at[1 - g], sem.at[1 - g]).start()

        @pl.when(jnp.logical_not(last(g)))
        def _():
            for source, target, sent, sem in pairs:
                pltpu.make_async_remote_copy(
                    src_ref=source,
                    dst_ref=target.at[g],
                    send_sem=sent.at[g],
                    recv_sem=sem.at[g],
                    device_id=(onward(g), position),
                    device_id_type=MESH,
                ).start()

    def hops(direction, part):
        return ring // 2 if direction == part % 2 else ring - 1 - ring // 2

    def behind(direction, k):
        return lax.rem(z + (ring - k if direction == 0 else k), ring)

    def ahead(direction):
        return at_z(1 if direction == 0 else ring - 1)

    def token_copy(g, direction, c, hop):
        block = tokens.at[g, c, behind(direction, hop)]
        return pltpu.make_async_remote_copy(
            src_ref=block,
            dst_ref=block,
            send_sem=token_send.at[g, direction, c, hop],
            recv_sem=token_recv.at[g, direction, c, hop],
            device_id=ahead(direction),
            device_id_type=MESH,
        )

    def compact(g, c):
        wait(landed.at[g, c], slab_recv.at[g, c])
        slot, row = iota((rows, slots), 1), iota((rows, slots), 0)
        inside = slot % SLAB
        keep = one_hot((row == slot // SLAB * CAP + inside) & (inside < CAP))
        tokens[g, c, z] = jnp.dot(
            keep, landed[g, c], preferred_element_type=F32
        ).astype(BF16)
        for direction in range(2):
            if hops(direction, c):
                token_copy(g, direction, c, 0).start()

    def token_stage(g, stage):
        for c in range(CHUNKS):
            for direction in range(2):
                if stage <= hops(direction, c):
                    wait(
                        tokens.at[g, c, behind(direction, stage)],
                        token_recv.at[g, direction, c, stage - 1],
                    )
                if stage < hops(direction, c):
                    token_copy(g, direction, c, stage).start()

    def hide(g, blocks):
        total = jnp.zeros((len(blocks) * rows, 2 * units), F32)
        for c in range(CHUNKS):
            parts = [tokens[g, c, block] for block in blocks]
            part = parts[0] if len(parts) == 1 else jnp.concatenate(parts, axis=0)
            total = total + lax.dot_general(
                part,
                gate_up[:, c * width : (c + 1) * width],
                (((1,), (1,)), ((), ())),
                preferred_element_type=F32,
            )
        units_out = (jax.nn.silu(total[:, :units]) * total[:, units:]).astype(BF16)
        for i, block in enumerate(blocks):
            start = pl.multiple_of(block * rows, 16)
            hidden_own[g, pl.ds(start, rows), :] = units_out[i * rows : (i + 1) * rows]

    def hide_stage(g, stage):
        if stage == 0:
            hide(g, [z])
        elif 2 * stage == ring:
            hide(g, [behind(0, stage)])
        else:
            hide(g, [behind(0, stage), behind(1, stage)])

    half_rows = ring * rows // 2

    def hidden_part(g, half, owner):
        lanes = pl.ds(pl.multiple_of(owner * units, units), units)
        return hidden.at[g, pl.ds(half * half_rows, half_rows), lanes]

    def hidden_copy_own(g):
        lanes = pl.ds(pl.multiple_of(z * units, units), units)
        return pltpu.make_async_copy(
            hidden_own.at[g], hidden.at[g, :, lanes], hidden_copy.at[g]
        )

    def hidden_ring(g, direction, half, hop):
        if hop == 0:
            source = hidden_own.at[g, pl.ds(half * half_rows, half_rows)]
        else:
            source = hidden_part(g, half, behind(direction, hop))
        return pltpu.make_async_remote_copy(
            src_ref=source,
            dst_ref=hidden_part(g, half, behind(direction, hop)),
            send_sem=hidden_send.at[g, direction, half, hop],
            recv_sem=hidden_recv.at[g, direction, half, hop],
            device_id=ahead(direction),
            device_id_type=MESH,
        )

    def hidden_stage(g, stage):
        for half in range(2):
            for direction in range(2):
                if 1 <= stage <= hops(direction, half):
                    wait(
                        hidden_part(g, half, behind(direction, stage)),
                        hidden_recv.at[g, direction, half, stage - 1],
                    )
                if stage < hops(direction, half):
                    hidden_ring(g, direction, half, stage).start()

    def project(g):
        hidden_copy_own(g).wait()
        for half in range(2):
            blocks = ring // 2
            result = jnp.dot(
                hidden[g, half * half_rows : (half + 1) * half_rows, :],
                down_w[...],
                preferred_element_type=F32,
            ).astype(BF16)
            for i in range(blocks):
                columns[g, half * blocks + i] = result[i * rows : (i + 1) * rows]
        pltpu.make_async_copy(
            columns.at[g, z], returned.at[g, z], columns_recv.at[g]
        ).start()

        @pl.loop(1, ring)
        def _(k):
            pltpu.make_async_remote_copy(
                src_ref=columns.at[g, lax.rem(z + k, ring)],
                dst_ref=returned.at[g, z],
                send_sem=columns_send.at[g],
                recv_sem=columns_recv.at[g],
                device_id=at_z(k),
                device_id_type=MESH,
            ).start()

    def give_back(g):
        wait(returned.at[g], columns_recv.at[g])
        slot, row = iota((slots, rows), 0), iota((slots, rows), 1)
        inside = slot % SLAB
        keep = one_hot((row == slot // SLAB * CAP + inside) & (inside < CAP))
        for k in range(ring // 2):
            parts = [
                jnp.dot(keep, returned[g, 2 * k + i], preferred_element_type=F32)
                for i in range(2)
            ]
            spread[g, k] = jnp.concatenate(parts, axis=1).astype(BF16)

        @pl.when(last(g))
        def _():
            pltpu.make_async_copy(
                spread.at[g, :, slab(y)], final.at[1 - g, :, slab(y)], final_recv.at[1 - g]
            ).start()

            @pl.loop(1, experts)
            def _(k):
                pltpu.make_async_remote_copy(
                    src_ref=spread.at[g, :, slab(lax.rem(y + k, experts))],
                    dst_ref=final.at[1 - g, :, slab(y)],
                    send_sem=final_send.at[g],
                    recv_sem=final_recv.at[1 - g],
                    device_id=at_y(k),
                    device_id_type=MESH,
                ).start()

        @pl.when(jnp.logical_not(last(g)))
        def _():
            pltpu.make_async_remote_copy(
                src_ref=spread.at[g, :, slab(y)],
                dst_ref=final.at[g, :, slab(y)],
                send_sem=final_send_same.at[g],
                recv_sem=final_recv.at[g],
                device_id=(onward(g), position),
                device_id_type=MESH,
            ).start()

            @pl.loop(1, experts)
            def _(k):
                target = lax.rem(y + k, experts)
                pltpu.make_async_remote_copy(
                    src_ref=spread.at[g, :, slab(target)],
                    dst_ref=final.at[g, :, slab(y)],
                    send_sem=final_send.at[g],
                    recv_sem=final_recv.at[g],
                    device_id=(onward(g), target * ring + z),
                    device_id_type=MESH,
                ).start()

    def combine(o):
        wait(residual.at[o], residual_recv.at[o])
        wait(mixing_here.at[o], mixing_recv.at[o])
        wait(final.at[o], final_recv.at[o])
        weights = mixing_here[o]
        picker = one_hot(weights != 0.0)
        weight = jnp.sum(weights, axis=-1, keepdims=True)
        span = final.shape[-1]
        for k in range(final.shape[1]):
            cut = slice(k * span, (k + 1) * span)
            picked = jnp.dot(picker, final[o, k], preferred_element_type=F32)
            outs[o][:, cut] = (residual[o, :, cut].astype(F32) + weight * picked).astype(BF16)

    normalize(0)
    picker = pick(0)
    mix(0)
    pl.semaphore_wait(barrier, greeted)
    for c in range(CHUNKS):
        dispatch(0, c, picker)
    normalize(1)
    picker = pick(1)
    mix(1)
    for c in range(CHUNKS):
        dispatch(1, c, picker)
    for g in range(2):
        send_residual(g)
    gate_up[:units] = gate_w[...]
    gate_up[units:] = up_w[...]

    for c in range(CHUNKS):
        compact(0, c)
    hide_stage(0, 0)
    final_stage = ring // 2
    for stage in range(1, final_stage):
        token_stage(0, stage)
        hide_stage(0, stage)
    for c in range(CHUNKS):
        compact(1, c)
    token_stage(0, final_stage)
    hide_stage(0, final_stage)
    hidden_copy_own(0).start()
    hidden_stage(0, 0)
    hide_stage(1, 0)
    for stage in range(1, final_stage):
        token_stage(1, stage)
        hidden_stage(0, stage)
        hide_stage(1, stage)
    hidden_stage(0, final_stage)
    project(0)
    token_stage(1, final_stage)
    hide_stage(1, final_stage)
    hidden_copy_own(1).start()
    hidden_stage(1, 0)
    hidden_stage(1, 1)
    give_back(0)
    for stage in range(2, final_stage + 1):
        hidden_stage(1, stage)
    project(1)
    give_back(1)
    combine(0)
    combine(1)

    for g in range(2):
        for c in range(CHUNKS):
            wait(slabs.at[g, c, : slots - SLAB], slab_send.at[g, c])
            for direction in range(2):
                for hop in range(hops(direction, c)):
                    wait(tokens.at[g, c, 0], token_send.at[g, direction, c, hop])
        for half in range(2):
            for direction in range(2):
                for hop in range(hops(direction, half)):
                    wait(hidden_part(g, half, 0), hidden_send.at[g, direction, half, hop])
        wait(columns.at[g, : ring - 1], columns_send.at[g])
        wait(spread.at[g, :, : slots - SLAB], final_send.at[g])

        @pl.when(jnp.logical_not(last(g)))
        def _(g=g):
            wait(spread.at[g, :, :SLAB], final_send_same.at[g])
            wait(residual.at[g], residual_send.at[g])
            wait(mixing.at[g], mixing_send.at[g])


def body(
    sections,
    act_down,
    act_up,
    norm_gain,
    gate_weight,
    up_weight,
    down_weight,
    routes_down,
    gates_down,
    routes_up,
    gates_up,
):
    count, depth = act_down.shape[1:]
    units = gate_weight.shape[1]
    hidden_units, piece = down_weight.shape[1:]
    ring = depth // piece
    rows, slots, width = EXPERTS * CAP, EXPERTS * SLAB, depth // CHUNKS
    half = -(-ring // 2)
    route_rows = jnp.concatenate([routes_down[0].T, routes_up[0].T], axis=0)
    dma = pltpu.SemaphoreType.DMA
    vmem = pl.BlockSpec(memory_space=pltpu.VMEM)
    outs = pl.pallas_call(
        functools.partial(kernel, EXPERTS, sections),
        out_shape=[jax.ShapeDtypeStruct((count, depth), BF16)] * 2,
        in_specs=[vmem] * 11,
        out_specs=[vmem] * 2,
        scratch_shapes=[
            pltpu.VMEM((2 * units, depth), BF16),
            pltpu.VMEM((2, count, depth), BF16),
            pltpu.VMEM((2, CHUNKS, slots, width), BF16),
            pltpu.VMEM((2, CHUNKS, slots, width), BF16),
            pltpu.VMEM((2, CHUNKS, ring, rows, width), BF16),
            pltpu.VMEM((2, ring * rows, units), BF16),
            pltpu.VMEM((2, ring * rows, hidden_units), BF16),
            pltpu.VMEM((2, ring, rows, piece), BF16),
            pltpu.VMEM((2, ring, rows, piece), BF16),
            pltpu.VMEM((2, ring // 2, slots, 2 * piece), BF16),
            pltpu.VMEM((2, ring // 2, slots, 2 * piece), BF16),
            pltpu.VMEM((2, count, depth), BF16),
            pltpu.VMEM((2, count, slots), F32),
            pltpu.VMEM((2, count, slots), F32),
            dma((2, CHUNKS)),
            dma((2, CHUNKS)),
            dma((2, 2, CHUNKS, half)),
            dma((2, 2, CHUNKS, half)),
            dma((2, 2, 2, half)),
            dma((2, 2, 2, half)),
            dma((2,)),
            dma((2,)),
            dma((2,)),
            dma((2,)),
            dma((2,)),
            dma((2,)),
            dma((2,)),
            dma((2,)),
            dma((2,)),
            dma((2,)),
        ],
        compiler_params=pltpu.CompilerParams(
            collective_id=0, has_side_effects=True, vmem_limit_bytes=56 * 1024 * 1024
        ),
    )(
        act_down[0],
        act_up[0],
        norm_gain,
        gate_weight[0],
        up_weight[0],
        down_weight[0],
        route_rows,
        routes_down[0],
        routes_up[0],
        gates_down[0],
        gates_up[0],
    )
    return tuple(out[None] for out in outs)


def solution(mesh):
    return jax.shard_map(
        functools.partial(body, mesh.shape["pipe"]),
        mesh=mesh,
        in_specs=(
            P("pipe", "expert", None),
            P("pipe", "expert", None),
            P("pipe", None),
            P("pipe", "expert", None),
            P("pipe", "expert", None),
            P("pipe", None, "expert"),
            P("pipe", "expert", None),
            P("pipe", "expert", None),
            P("pipe", "expert", None),
            P("pipe", "expert", None),
        ),
        out_specs=(P("pipe", "expert", None), P("pipe", "expert", None)),
        check_vma=False,
    )
```

```python
import functools

import jax
import jax.numpy as jnp
from jax import lax
from jax.experimental import pallas as pl
from jax.experimental.pallas import tpu as pltpu
from jax.sharding import PartitionSpec as P

EXPERTS = 8
CAP = 10
SLAB = 16
FOLD = 4
OFFSET = 1
EPSILON = 1e-06

MESH = pl.DeviceIdType.MESH
F32 = jnp.float32
BF16 = jnp.bfloat16


def one_hot(condition):
    return jnp.where(condition, 1.0, 0.0).astype(BF16)


def iota(shape, dimension):
    return lax.broadcasted_iota(jnp.int32, shape, dimension)


def dot_t(a, b):
    return lax.dot_general(a, b, (((1,), (1,)), ((), ())), preferred_element_type=F32)


def kernel(
    experts,
    sections,
    x_down,
    x_up,
    gain,
    routes_down,
    routes_up,
    gates_down,
    gates_up,
    gate_w,
    up_w,
    down_w,
    out_down,
    out_up,
    gate_up,
    down,
    normed,
    slabs,
    landed,
    tokens,
    hidden_own,
    hidden,
    columns,
    returned,
    spread,
    final,
    residual,
    notes,
    notes_here,
    weight_copy,
    slab_send,
    slab_recv,
    token_send,
    token_recv,
    hidden_send,
    hidden_recv,
    hidden_copy,
    columns_send,
    columns_recv,
    final_send,
    final_send_same,
    final_recv,
    residual_send,
    residual_recv,
    notes_send,
    notes_recv,
):
    groups, ring = tokens.shape[:2]
    per = SLAB // FOLD
    rows = experts * per
    slots = experts * SLAB
    count, depth = x_down.shape
    width = depth // FOLD
    units = gate_w.shape[0]
    pipe = lax.axis_index("pipe")
    position = lax.axis_index("expert")
    y = position // ring
    z = position % ring
    x_refs = (x_down, x_up)
    routes = (routes_down, routes_up)
    gates = (gates_down, gates_up)
    outs = (out_down, out_up)

    def groups_of(stream):
        return range(stream * CAP // per, -(-(stream + 1) * CAP // per))

    def streams_of(g):
        return [stream for stream in range(2) if g in groups_of(stream)]

    def at_y(k):
        return (pipe, lax.rem(y + k, experts) * ring + z)

    def at_z(k):
        return (pipe, y * ring + lax.rem(z + k, ring))

    barrier = pltpu.get_barrier_semaphore()

    def greet(device):
        pl.semaphore_signal(barrier, inc=1, device_id=device, device_id_type=MESH)

    @pl.loop(1, experts)
    def _(k):
        greet(at_y(k))

    @pl.loop(1, ring)
    def _(k):
        greet(at_z(k))

    @pl.when(pipe > 0)
    def _():
        @pl.loop(0, experts)
        def _(k):
            greet((pipe - 1, k * ring + z))

    @pl.when(pipe < sections - 1)
    def _():
        @pl.loop(0, experts)
        def _(k):
            greet((pipe + 1, k * ring + z))

    neighbours = jnp.where(pipe > 0, 1, 0) + jnp.where(pipe < sections - 1, 1, 0)
    greeted = experts - 1 + ring - 1 + experts * neighbours

    weight_copies = (
        pltpu.make_async_copy(gate_w, gate_up.at[:units], weight_copy.at[0]),
        pltpu.make_async_copy(up_w, gate_up.at[units:], weight_copy.at[1]),
        pltpu.make_async_copy(down_w, down, weight_copy.at[2]),
    )
    for copy in weight_copies:
        copy.start()

    def wait(ref, sem):
        pltpu.make_async_copy(ref, ref, sem).wait()

    def remote(source, target, sent, received, device):
        return pltpu.make_async_remote_copy(
            src_ref=source,
            dst_ref=target,
            send_sem=sent,
            recv_sem=received,
            device_id=device,
            device_id_type=MESH,
        )

    def normalize(stream):
        x_ref = x_refs[stream]
        total = jnp.zeros((count, 1), F32)
        for c in range(FOLD):
            part = x_ref[:, c * width : (c + 1) * width].astype(F32)
            total = total + jnp.sum(part * part, axis=-1, keepdims=True)
        inverse = lax.rsqrt(total / depth + EPSILON)
        for c in range(FOLD):
            cut = slice(c * width, (c + 1) * width)
            part = x_ref[:, cut].astype(F32)
            normed[stream, :, cut] = (part * inverse * gain[:, cut].astype(F32)).astype(BF16)

    def number(stream):
        named = one_hot(routes[stream][...] == iota((experts, count), 0))
        earlier = one_hot(iota((count, count), 0) < iota((count, count), 1))
        rank = jnp.dot(named, earlier, preferred_element_type=F32)
        slot = jnp.sum(named.astype(F32) * rank, axis=0, keepdims=True) + stream * CAP
        expert = routes[stream][...].astype(F32)
        row = iota((128, count), 0)
        table = jnp.where(row == 0, expert, jnp.where(row == 1, slot, gates[stream][...]))
        notes[stream] = jnp.transpose(table)
        return expert, slot

    def slab(k):
        return pl.ds(pl.multiple_of(k * SLAB, SLAB), SLAB)

    def matches(g, place, expert, slot):
        inside = place % per + g * per
        return (expert == (place // SLAB).astype(F32)) & (slot == inside.astype(F32))

    def dispatch(g, numbers):
        place = iota((slots, count), 0)
        total = jnp.zeros((slots, width), F32)
        for stream in streams_of(g):
            chosen = matches(g, place, *numbers[stream])
            for c in range(FOLD):
                total = total + jnp.dot(
                    one_hot(chosen & (place // per % FOLD == c)),
                    normed[stream, :, c * width : (c + 1) * width],
                    preferred_element_type=F32,
                )
        slabs[g] = total.astype(BF16)
        pltpu.make_async_copy(
            slabs.at[g, slab(y)], landed.at[g, slab(y)], slab_recv.at[g]
        ).start()

        @pl.loop(1, experts)
        def _(k):
            remote(
                slabs.at[g, slab(lax.rem(y + k, experts))],
                landed.at[g, slab(y)],
                slab_send.at[g],
                slab_recv.at[g],
                at_y(k),
            ).start()

    def last(stream):
        return pipe == (sections - 1 if stream == 0 else 0)

    def onward(stream):
        return pipe + 1 if stream == 0 else pipe - 1

    def send_residual(stream):
        pairs = (
            (x_refs[stream], residual, residual_send, residual_recv),
            (notes.at[stream], notes_here, notes_send, notes_recv),
        )

        @pl.when(last(stream))
        def _():
            for source, target, _, sem in pairs:
                end = 1 - stream
                pltpu.make_async_copy(source, target.at[end], sem.at[end]).start()

        @pl.when(jnp.logical_not(last(stream)))
        def _():
            for source, target, sent, sem in pairs:
                remote(
                    source,
                    target.at[stream],
                    sent.at[stream],
                    sem.at[stream],
                    (onward(stream), position),
                ).start()

    def hops(direction, part):
        return ring // 2 if direction == part % 2 else ring - 1 - ring // 2

    def behind(direction, k):
        return lax.rem(z + (ring - k if direction == 0 else k), ring)

    def ahead(direction):
        return at_z(1 if direction == 0 else ring - 1)

    half = FOLD * rows // 2

    def token_part(g, part, owner):
        return tokens.at[g, owner, part * half : (part + 1) * half]

    def token_ring(g, part, direction, hop):
        block = token_part(g, part, behind(direction, hop))
        return remote(
            block,
            block,
            token_send.at[g, part, direction, hop],
            token_recv.at[g, part, direction, hop],
            ahead(direction),
        )

    def token_stage(g, stage):
        for part in range(2):
            for direction in range(2):
                if 1 <= stage <= hops(direction, part):
                    wait(
                        token_part(g, part, behind(direction, stage)),
                        token_recv.at[g, part, direction, stage - 1],
                    )
                if stage < hops(direction, part):
                    token_ring(g, part, direction, stage).start()

    def compact(g):
        wait(landed.at[g], slab_recv.at[g])
        size = FOLD * rows
        row, place = iota((size, slots), 0), iota((size, slots), 1)
        same = row // rows == place // per % FOLD
        same = same & (row % rows == place // SLAB * per + place % per)
        tokens[g, z] = jnp.dot(
            one_hot(same), landed[g], preferred_element_type=F32
        ).astype(BF16)

    def hide(g):
        total = jnp.zeros((ring * rows, 2 * units), F32)
        for c in range(FOLD):
            part = tokens[g, :, c * rows : (c + 1) * rows, :].reshape(ring * rows, width)
            total = total + dot_t(part, gate_up[:, c * width : (c + 1) * width])
        hidden_own[g] = (jax.nn.silu(total[:, :units]) * total[:, units:]).astype(BF16)

    def hidden_part(g, owner):
        return hidden.at[g, :, pl.ds(pl.multiple_of(owner * units, units), units)]

    def hidden_copy_own(g):
        return pltpu.make_async_copy(hidden_own.at[g], hidden_part(g, z), hidden_copy.at[g])

    def hidden_stage(g, stage):
        if stage == 0:
            hidden_copy_own(g).start()
        for direction in range(2):
            if 1 <= stage <= hops(direction, g):
                wait(
                    hidden_part(g, behind(direction, stage)),
                    hidden_recv.at[g, direction, stage - 1],
                )
            if stage < hops(direction, g):
                block = hidden_part(g, behind(direction, stage))
                remote(
                    hidden_own.at[g] if stage == 0 else block,
                    block,
                    hidden_send.at[g, direction, stage],
                    hidden_recv.at[g, direction, stage],
                    ahead(direction),
                ).start()

    def project(g):
        hidden_copy_own(g).wait()
        result = dot_t(hidden[g], down[...]).astype(BF16)
        piece = rows // 2
        for b in range(ring):
            first, second = (
                result[(2 * b + i) * piece : (2 * b + i + 1) * piece] for i in range(2)
            )
            columns[g, b] = jnp.concatenate([first, second], axis=1)
        target = returned.at[g, z % 2, z // 2]
        pltpu.make_async_copy(columns.at[g, z], target, columns_recv.at[g]).start()

        @pl.loop(1, ring)
        def _(k):
            remote(
                columns.at[g, lax.rem(z + k, ring)],
                target,
                columns_send.at[g],
                columns_recv.at[g],
                at_z(k),
            ).start()

    def give_back(g):
        wait(returned.at[g], columns_recv.at[g])
        size, piece = slots // 2, rows // 2
        row, place = iota((size, size), 0), iota((size, size), 1)
        same = row // per % FOLD == place // piece
        same = same & (row // SLAB * per + row % per == place % piece)
        order = one_hot(same)
        even, odd = (
            jnp.dot(
                order,
                returned[g, i].reshape(size, width),
                preferred_element_type=F32,
            )
            for i in range(2)
        )
        cut = width // 2
        for i in range(2):
            lanes = slice(i * cut, (i + 1) * cut)
            joined = jnp.concatenate([even[:, lanes], odd[:, lanes]], axis=1)
            spread[g, i * size : (i + 1) * size] = joined.astype(BF16)
        for stream in streams_of(g):
            send_back(g, stream)

    def send_back(g, stream):
        index = g - groups_of(stream)[0]

        @pl.when(last(stream))
        def _():
            end = 1 - stream
            target = final.at[end, index, slab(y)]
            pltpu.make_async_copy(
                spread.at[g, slab(y)], target, final_recv.at[end, index]
            ).start()

            @pl.loop(1, experts)
            def _(k):
                remote(
                    spread.at[g, slab(lax.rem(y + k, experts))],
                    target,
                    final_send.at[stream, index],
                    final_recv.at[end, index],
                    at_y(k),
                ).start()

        @pl.when(jnp.logical_not(last(stream)))
        def _():
            target = final.at[stream, index, slab(y)]
            remote(
                spread.at[g, slab(y)],
                target,
                final_send_same.at[stream, index],
                final_recv.at[stream, index],
                (onward(stream), position),
            ).start()

            @pl.loop(1, experts)
            def _(k):
                to = lax.rem(y + k, experts)
                remote(
                    spread.at[g, slab(to)],
                    target,
                    final_send.at[stream, index],
                    final_recv.at[stream, index],
                    (onward(stream), to * ring + z),
                ).start()

    def combine(end):
        wait(residual.at[end], residual_recv.at[end])
        wait(notes_here.at[end], notes_recv.at[end])
        place = iota((count, slots), 1)
        note = notes_here[end]
        expert, slot, weight = note[:, 0:1], note[:, 1:2], note[:, 2:3]
        turned = jnp.where(pipe == 0, end == 0, (pipe == sections - 1) & (end == 1))
        stream = jnp.where(turned, 1 - end, end)
        start = stream * CAP // per * per
        chosen = []
        for index in range(len(groups_of(0))):
            wait(final.at[end, index], final_recv.at[end, index])
            inside = place % per + index * per + start
            chosen.append(
                (expert == (place // SLAB).astype(F32)) & (slot == inside.astype(F32))
            )
        for c in range(FOLD):
            cut = slice(c * width, (c + 1) * width)
            picked = jnp.zeros((count, width), F32)
            for index, choice in enumerate(chosen):
                picked = picked + jnp.dot(
                    one_hot(choice & (place // per % FOLD == c)),
                    final[end, index],
                    preferred_element_type=F32,
                )
            outs[end][:, cut] = (residual[end, :, cut].astype(F32) + weight * picked).astype(BF16)

    numbers = [None, None]
    for stream in range(2):
        normalize(stream)
        numbers[stream] = number(stream)
        if stream == 0:
            pl.semaphore_wait(barrier, greeted)
        for g in range(groups):
            if streams_of(g)[-1] == stream:
                dispatch(g, numbers)
        send_residual(stream)
    for copy in weight_copies:
        copy.wait()

    stages = ring // 2

    def action(g, step):
        if step == 0:
            compact(g)
        if step <= stages:
            token_stage(g, step)
        if step == stages:
            hide(g)
        if stages <= step <= 2 * stages:
            hidden_stage(g, step - stages)
        if step == 2 * stages:
            project(g)
        if step == 2 * stages + 1:
            give_back(g)

    final_step = 2 * stages + 1
    for step in range((groups - 1) * OFFSET + final_step + 1):
        for g in range(groups):
            if 0 <= step - g * OFFSET <= final_step:
                action(g, step - g * OFFSET)
    combine(0)
    combine(1)

    for g in range(groups):
        wait(slabs.at[g, : slots - SLAB], slab_send.at[g])
        for direction in range(2):
            for part in range(2):
                for hop in range(hops(direction, part)):
                    wait(token_part(g, part, 0), token_send.at[g, part, direction, hop])
            for hop in range(hops(direction, g)):
                wait(hidden_own.at[g], hidden_send.at[g, direction, hop])
        wait(columns.at[g, : ring - 1], columns_send.at[g])
    for stream in range(2):
        for index in range(len(groups_of(stream))):
            wait(spread.at[0, : slots - SLAB], final_send.at[stream, index])

        @pl.when(jnp.logical_not(last(stream)))
        def _(stream=stream):
            for index in range(len(groups_of(stream))):
                wait(spread.at[0, :SLAB], final_send_same.at[stream, index])
            wait(residual.at[stream], residual_send.at[stream])
            wait(notes.at[stream], notes_send.at[stream])


def body(
    sections,
    act_down,
    act_up,
    norm_gain,
    gate_weight,
    up_weight,
    down_weight,
    routes_down,
    gates_down,
    routes_up,
    gates_up,
):
    count, depth = act_down.shape[1:]
    units = gate_weight.shape[1]
    hidden_units, piece = down_weight.shape[1:]
    ring = depth // piece
    per = SLAB // FOLD
    groups = 2 * CAP // per
    mine = -(-CAP // per)
    rows, slots, width = EXPERTS * per, EXPERTS * SLAB, depth // FOLD
    half = ring // 2
    dma = pltpu.SemaphoreType.DMA
    vmem = pl.BlockSpec(memory_space=pltpu.VMEM)
    anywhere = pl.BlockSpec(memory_space=pl.ANY)
    outs = pl.pallas_call(
        functools.partial(kernel, EXPERTS, sections),
        out_shape=[jax.ShapeDtypeStruct((count, depth), BF16)] * 2,
        in_specs=[vmem] * 7 + [anywhere] * 3,
        out_specs=[vmem] * 2,
        scratch_shapes=[
            pltpu.VMEM((2 * units, depth), BF16),
            pltpu.VMEM((piece, hidden_units), BF16),
            pltpu.VMEM((2, count, depth), BF16),
            pltpu.VMEM((groups, slots, width), BF16),
            pltpu.VMEM((groups, slots, width), BF16),
            pltpu.VMEM((groups, ring, FOLD * rows, width), BF16),
            pltpu.VMEM((groups, ring * rows, units), BF16),
            pltpu.VMEM((groups, ring * rows, hidden_units), BF16),
            pltpu.VMEM((groups, ring, rows // 2, 2 * piece), BF16),
            pltpu.VMEM((groups, 2, ring // 2, rows // 2, 2 * piece), BF16),
            pltpu.VMEM((groups, slots, width), BF16),
            pltpu.VMEM((2, mine, slots, width), BF16),
            pltpu.VMEM((2, count, depth), BF16),
            pltpu.VMEM((2, count, 128), F32),
            pltpu.VMEM((2, count, 128), F32),
            dma((3,)),
            dma((groups,)),
            dma((groups,)),
            dma((groups, 2, 2, half)),
            dma((groups, 2, 2, half)),
            dma((groups, 2, half)),
            dma((groups, 2, half)),
            dma((groups,)),
            dma((groups,)),
            dma((groups,)),
            dma((2, mine)),
            dma((2, mine)),
            dma((2, mine)),
            dma((2,)),
            dma((2,)),
            dma((2,)),
            dma((2,)),
        ],
        compiler_params=pltpu.CompilerParams(
            collective_id=0, has_side_effects=True, vmem_limit_bytes=56 * 1024 * 1024
        ),
    )(
        act_down[0],
        act_up[0],
        norm_gain,
        routes_down[0].T,
        routes_up[0].T,
        gates_down[0].T,
        gates_up[0].T,
        gate_weight[0],
        up_weight[0],
        down_weight[0].T,
    )
    return tuple(out[None] for out in outs)


def solution(mesh):
    return jax.shard_map(
        functools.partial(body, mesh.shape["pipe"]),
        mesh=mesh,
        in_specs=(
            P("pipe", "expert", None),
            P("pipe", "expert", None),
            P("pipe", None),
            P("pipe", "expert", None),
            P("pipe", "expert", None),
            P("pipe", None, "expert"),
            P("pipe", "expert", None),
            P("pipe", "expert", None),
            P("pipe", "expert", None),
            P("pipe", "expert", None),
        ),
        out_specs=(P("pipe", "expert", None), P("pipe", "expert", None)),
        check_vma=False,
    )
```

```python
import functools

import jax
import jax.numpy as jnp
from jax import lax
from jax.experimental import pallas as pl
from jax.experimental.pallas import tpu as pltpu
from jax.sharding import PartitionSpec as P

EXPERTS = 8
CAP = 10
SLAB = 16
FOLD = 4
OFFSET = 1
EPSILON = 1e-06

MESH = pl.DeviceIdType.MESH
F32 = jnp.float32
BF16 = jnp.bfloat16


def one_hot(condition):
    return jnp.where(condition, 1.0, 0.0).astype(BF16)


def iota(shape, dimension):
    return lax.broadcasted_iota(jnp.int32, shape, dimension)


def dot_t(a, b):
    return lax.dot_general(a, b, (((1,), (1,)), ((), ())), preferred_element_type=F32)


def kernel(
    experts,
    sections,
    x_down,
    x_up,
    gain,
    routes_down,
    routes_up,
    gates_down,
    gates_up,
    gate_w,
    up_w,
    down_w,
    out_down,
    out_up,
    gate_up,
    down,
    normed,
    raw,
    table,
    tables,
    slabs_raw,
    landed_raw,
    slabs,
    landed,
    tokens,
    hidden_own,
    hidden,
    columns,
    returned,
    spread,
    final,
    residual,
    notes,
    notes_here,
    sums,
    weight_copy,
    raw_send,
    raw_recv,
    table_send,
    table_recv,
    slab_raw_send,
    slab_raw_recv,
    slab_send,
    slab_recv,
    token_send,
    token_recv,
    hidden_send,
    hidden_recv,
    hidden_copy,
    columns_send,
    columns_recv,
    final_send,
    final_send_same,
    final_recv,
    residual_send,
    residual_recv,
    notes_send,
    notes_recv,
):
    groups, ring = tokens.shape[:2]
    per = SLAB // FOLD
    rows = experts * per
    slots = experts * SLAB
    count, depth = x_down.shape
    width = depth // FOLD
    units = gate_w.shape[0]
    pipe = lax.axis_index("pipe")
    position = lax.axis_index("expert")
    y = position // ring
    z = position % ring
    x_refs = (x_down, x_up)
    routes = (routes_down, routes_up)
    gates = (gates_down, gates_up)
    outs = (out_down, out_up)

    def groups_of(stream):
        return range(stream * CAP // per, -(-(stream + 1) * CAP // per))

    def streams_of(g):
        return [stream for stream in range(2) if g in groups_of(stream)]

    def at_y(k):
        return (pipe, lax.rem(y + k, experts) * ring + z)

    def at_z(k):
        return (pipe, y * ring + lax.rem(z + k, ring))

    barrier = pltpu.get_barrier_semaphore()

    def greet(device):
        pl.semaphore_signal(barrier, inc=1, device_id=device, device_id_type=MESH)

    @pl.loop(1, experts)
    def _(k):
        greet(at_y(k))

    @pl.loop(1, ring)
    def _(k):
        greet(at_z(k))

    @pl.when(pipe > 0)
    def _():
        @pl.loop(0, experts)
        def _(k):
            greet((pipe - 1, k * ring + z))

    @pl.when(pipe < sections - 1)
    def _():
        @pl.loop(0, experts)
        def _(k):
            greet((pipe + 1, k * ring + z))

    neighbours = jnp.where(pipe > 0, 1, 0) + jnp.where(pipe < sections - 1, 1, 0)
    greeted = experts - 1 + ring - 1 + experts * neighbours

    weight_copies = (
        pltpu.make_async_copy(gate_w, gate_up.at[:units], weight_copy.at[0]),
        pltpu.make_async_copy(up_w, gate_up.at[units:], weight_copy.at[1]),
        pltpu.make_async_copy(down_w, down, weight_copy.at[2]),
    )
    for copy in weight_copies:
        copy.start()

    def wait(ref, sem):
        pltpu.make_async_copy(ref, ref, sem).wait()

    def remote(source, target, sent, received, device):
        return pltpu.make_async_remote_copy(
            src_ref=source,
            dst_ref=target,
            send_sem=sent,
            recv_sem=received,
            device_id=device,
            device_id_type=MESH,
        )

    def normalize(stream):
        x_ref = x_refs[stream]
        total = jnp.zeros((count, 1), F32)
        for c in range(FOLD):
            part = x_ref[:, c * width : (c + 1) * width].astype(F32)
            total = total + jnp.sum(part * part, axis=-1, keepdims=True)
        inverse = lax.rsqrt(total / depth + EPSILON)
        for c in range(FOLD):
            cut = slice(c * width, (c + 1) * width)
            part = x_ref[:, cut].astype(F32)
            scaled = (part * inverse * gain[:, cut].astype(F32)).astype(BF16)
            if c == 0:
                raw[z, stream * count : (stream + 1) * count] = scaled
            else:
                normed[stream, :, cut] = scaled

    def number(stream):
        named = one_hot(routes[stream][...] == iota((experts, count), 0))
        earlier = one_hot(iota((count, count), 0) < iota((count, count), 1))
        rank = jnp.dot(named, earlier, preferred_element_type=F32)
        slot = jnp.sum(named.astype(F32) * rank, axis=0, keepdims=True) + stream * CAP
        expert = routes[stream][...].astype(F32)
        row = iota((128, count), 0)
        note = jnp.where(row == 0, expert, jnp.where(row == 1, slot, gates[stream][...]))
        notes[stream] = jnp.transpose(note)
        return expert, slot

    def send_table(numbers):
        row = iota((8, 2 * count), 0)
        expert, slot = (jnp.concatenate(pair, axis=1) for pair in zip(*numbers))
        table[...] = jnp.where(row == 0, expert, slot)
        target = tables.at[:, pl.ds(pl.multiple_of(z * 2 * count, 2 * count), 2 * count)]
        pltpu.make_async_copy(table, target, table_recv).start()

        @pl.loop(1, ring)
        def _(k):
            remote(table, target, table_send, table_recv, at_z(k)).start()

    def slab(k):
        return pl.ds(pl.multiple_of(k * SLAB, SLAB), SLAB)

    def matches(g, place, expert, slot):
        inside = place % per + g * per
        return (expert == (place // SLAB).astype(F32)) & (slot == inside.astype(F32))

    def pack(g, numbers):
        place = iota((slots, count), 0)
        total = jnp.zeros((slots, width), F32)
        for stream in streams_of(g):
            chosen = matches(g, place, *numbers[stream])
            for c in range(1, FOLD):
                total = total + jnp.dot(
                    one_hot(chosen & (place // per % FOLD == c)),
                    normed[stream, :, c * width : (c + 1) * width],
                    preferred_element_type=F32,
                )
        slabs[g] = total.astype(BF16)

    def dispatch(g):
        pltpu.make_async_copy(
            slabs.at[g, slab(y)], landed.at[g, slab(y)], slab_recv.at[g]
        ).start()

        @pl.loop(1, experts)
        def _(k):
            remote(
                slabs.at[g, slab(lax.rem(y + k, experts))],
                landed.at[g, slab(y)],
                slab_send.at[g],
                slab_recv.at[g],
                at_y(k),
            ).start()

    def last(stream):
        return pipe == (sections - 1 if stream == 0 else 0)

    def onward(stream):
        return pipe + 1 if stream == 0 else pipe - 1

    def send_residual(stream):
        pairs = (
            (x_refs[stream], residual, residual_send, residual_recv),
            (notes.at[stream], notes_here, notes_send, notes_recv),
        )

        @pl.when(last(stream))
        def _():
            for source, target, _, sem in pairs:
                end = 1 - stream
                pltpu.make_async_copy(source, target.at[end], sem.at[end]).start()

        @pl.when(jnp.logical_not(last(stream)))
        def _():
            for source, target, sent, sem in pairs:
                remote(
                    source,
                    target.at[stream],
                    sent.at[stream],
                    sem.at[stream],
                    (onward(stream), position),
                ).start()

    def hops(direction, part):
        return ring // 2 if direction == part % 2 else ring - 1 - ring // 2

    def behind(direction, k):
        return lax.rem(z + (ring - k if direction == 0 else k), ring)

    def ahead(direction):
        return at_z(1 if direction == 0 else ring - 1)

    half = (FOLD - 1) * rows // 2

    def raw_ring(part, direction, hop):
        block = raw.at[behind(direction, hop), part * count : (part + 1) * count]
        return remote(
            block,
            block,
            raw_send.at[part, direction, hop],
            raw_recv.at[part, direction, hop],
            ahead(direction),
        )

    def raw_stage(part, stage):
        for direction in range(2):
            if 1 <= stage <= hops(direction, part):
                wait(
                    raw.at[behind(direction, stage), part * count : (part + 1) * count],
                    raw_recv.at[part, direction, stage - 1],
                )
            if stage < hops(direction, part):
                raw_ring(part, direction, stage).start()

    def dispatch_raw(g):
        if g == 0:
            wait(tables, table_recv)
        size, span = ring * rows, ring * 2 * count
        row, lane = iota((size, span), 0), iota((size, span), 1)
        inside = row % per + g * per
        chosen = tables[0:1, :] == (row // (ring * per)).astype(F32)
        chosen = chosen & (tables[1:2, :] == inside.astype(F32))
        chosen = chosen & (row // per % ring == lane // (2 * count))
        slabs_raw[g] = jnp.dot(
            one_hot(chosen), raw[...].reshape(span, width), preferred_element_type=F32
        ).astype(BF16)

        def part(k):
            return pl.ds(pl.multiple_of(k * ring * per, ring * per), ring * per)

        pltpu.make_async_copy(
            slabs_raw.at[g, part(y)], landed_raw.at[g, part(y)], slab_raw_recv.at[g]
        ).start()

        @pl.loop(1, experts)
        def _(k):
            remote(
                slabs_raw.at[g, part(lax.rem(y + k, experts))],
                landed_raw.at[g, part(y)],
                slab_raw_send.at[g],
                slab_raw_recv.at[g],
                at_y(k),
            ).start()

    def token_part(g, part, owner):
        return tokens.at[g, owner, part * half : (part + 1) * half]

    def token_ring(g, part, direction, hop):
        block = token_part(g, part, behind(direction, hop))
        return remote(
            block,
            block,
            token_send.at[g, part, direction, hop],
            token_recv.at[g, part, direction, hop],
            ahead(direction),
        )

    def token_stage(g, stage):
        for part in range(2):
            for direction in range(2):
                if 1 <= stage <= hops(direction, part):
                    wait(
                        token_part(g, part, behind(direction, stage)),
                        token_recv.at[g, part, direction, stage - 1],
                    )
                if stage < hops(direction, part):
                    token_ring(g, part, direction, stage).start()

    def compact(g):
        wait(landed.at[g], slab_recv.at[g])
        size = (FOLD - 1) * rows
        row, place = iota((size, slots), 0), iota((size, slots), 1)
        same = row // rows + 1 == place // per % FOLD
        same = same & (row % rows == place // SLAB * per + place % per)
        tokens[g, z] = jnp.dot(
            one_hot(same), landed[g], preferred_element_type=F32
        ).astype(BF16)

    def hide(g):
        wait(landed_raw.at[g], slab_raw_recv.at[g])
        size = ring * rows
        row, place = iota((size, size), 0), iota((size, size), 1)
        same = (row // rows == place // per % ring) & (row % per == place % per)
        same = same & (row // per % experts == place // (ring * per))
        part = jnp.dot(one_hot(same), landed_raw[g], preferred_element_type=F32)
        total = dot_t(part.astype(BF16), gate_up[:, :width])
        for c in range(1, FOLD):
            part = tokens[g, :, (c - 1) * rows : c * rows, :].reshape(size, width)
            total = total + dot_t(part, gate_up[:, c * width : (c + 1) * width])
        hidden_own[g] = (jax.nn.silu(total[:, :units]) * total[:, units:]).astype(BF16)

    def hidden_part(g, owner):
        return hidden.at[g, :, pl.ds(pl.multiple_of(owner * units, units), units)]

    def hidden_copy_own(g):
        return pltpu.make_async_copy(hidden_own.at[g], hidden_part(g, z), hidden_copy.at[g])

    def hidden_stage(g, stage):
        if stage == 0:
            hidden_copy_own(g).start()
        for direction in range(2):
            if 1 <= stage <= hops(direction, g):
                wait(
                    hidden_part(g, behind(direction, stage)),
                    hidden_recv.at[g, direction, stage - 1],
                )
            if stage < hops(direction, g):
                block = hidden_part(g, behind(direction, stage))
                remote(
                    hidden_own.at[g] if stage == 0 else block,
                    block,
                    hidden_send.at[g, direction, stage],
                    hidden_recv.at[g, direction, stage],
                    ahead(direction),
                ).start()

    def project(g):
        hidden_copy_own(g).wait()
        result = dot_t(hidden[g], down[...]).astype(BF16)
        piece = rows // 2
        for b in range(ring):
            first, second = (
                result[(2 * b + i) * piece : (2 * b + i + 1) * piece] for i in range(2)
            )
            columns[g, b] = jnp.concatenate([first, second], axis=1)
        target = returned.at[g, z % 2, z // 2]
        pltpu.make_async_copy(columns.at[g, z], target, columns_recv.at[g]).start()

        @pl.loop(1, ring)
        def _(k):
            remote(
                columns.at[g, lax.rem(z + k, ring)],
                target,
                columns_send.at[g],
                columns_recv.at[g],
                at_z(k),
            ).start()

    def give_back(g):
        wait(returned.at[g], columns_recv.at[g])
        size, piece = slots // 2, rows // 2
        row, place = iota((size, size), 0), iota((size, size), 1)
        same = row // per % FOLD == place // piece
        same = same & (row // SLAB * per + row % per == place % piece)
        order = one_hot(same)
        even, odd = (
            jnp.dot(
                order,
                returned[g, i].reshape(size, width),
                preferred_element_type=F32,
            )
            for i in range(2)
        )
        cut = width // 2
        for i in range(2):
            lanes = slice(i * cut, (i + 1) * cut)
            joined = jnp.concatenate([even[:, lanes], odd[:, lanes]], axis=1)
            spread[g, i * size : (i + 1) * size] = joined.astype(BF16)
        for stream in streams_of(g):
            send_back(g, stream)

    def send_back(g, stream):
        index = g - groups_of(stream)[0]

        @pl.when(last(stream))
        def _():
            end = 1 - stream
            target = final.at[end, index, slab(y)]
            pltpu.make_async_copy(
                spread.at[g, slab(y)], target, final_recv.at[end, index]
            ).start()

            @pl.loop(1, experts)
            def _(k):
                remote(
                    spread.at[g, slab(lax.rem(y + k, experts))],
                    target,
                    final_send.at[stream, index],
                    final_recv.at[end, index],
                    at_y(k),
                ).start()

        @pl.when(jnp.logical_not(last(stream)))
        def _():
            target = final.at[stream, index, slab(y)]
            remote(
                spread.at[g, slab(y)],
                target,
                final_send_same.at[stream, index],
                final_recv.at[stream, index],
                (onward(stream), position),
            ).start()

            @pl.loop(1, experts)
            def _(k):
                to = lax.rem(y + k, experts)
                remote(
                    spread.at[g, slab(to)],
                    target,
                    final_send.at[stream, index],
                    final_recv.at[stream, index],
                    (onward(stream), to * ring + z),
                ).start()

    def combine(end, index):
        if index == 0:
            wait(residual.at[end], residual_recv.at[end])
            wait(notes_here.at[end], notes_recv.at[end])
        wait(final.at[end, index], final_recv.at[end, index])
        place = iota((count, slots), 1)
        note = notes_here[end]
        expert, slot, weight = note[:, 0:1], note[:, 1:2], note[:, 2:3]
        turned = jnp.where(pipe == 0, end == 0, (pipe == sections - 1) & (end == 1))
        stream = jnp.where(turned, 1 - end, end)
        inside = place % per + index * per + stream * CAP // per * per
        chosen = (expert == (place // SLAB).astype(F32)) & (slot == inside.astype(F32))
        for c in range(FOLD):
            cut = slice(c * width, (c + 1) * width)
            picked = jnp.dot(
                one_hot(chosen & (place // per % FOLD == c)),
                final[end, index],
                preferred_element_type=F32,
            )
            if index > 0:
                picked = picked + sums[end, :, cut]
            if index < len(groups_of(0)) - 1:
                sums[end, :, cut] = picked
            else:
                total = residual[end, :, cut].astype(F32) + weight * picked
                outs[end][:, cut] = total.astype(BF16)

    normalize(0)
    numbers = [number(0)]
    pack(0, numbers)
    pl.semaphore_wait(barrier, greeted)
    raw_stage(0, 0)
    dispatch(0)
    normalize(1)
    raw_stage(1, 0)
    numbers.append(number(1))
    send_table(numbers)
    for g in range(1, groups):
        pack(g, numbers)
        dispatch(g)
    for stream in range(2):
        send_residual(stream)
    for copy in weight_copies:
        copy.wait()

    stages = ring // 2
    final_step = 2 * stages + 1

    def action(g, step):
        if step == 0:
            compact(g)
        if step <= stages:
            token_stage(g, step)
        if step == stages:
            hide(g)
        if stages <= step <= 2 * stages:
            hidden_stage(g, step - stages)
        if step == 2 * stages:
            project(g)
        if step == final_step:
            give_back(g)

    for step in range(1, (groups - 1) * OFFSET + final_step + 2):
        if step <= stages:
            for part in range(2):
                raw_stage(part, step)
        if 0 <= step - stages < groups:
            dispatch_raw(step - stages)
        for g in range(groups):
            if 0 <= step - 1 - g * OFFSET <= final_step:
                action(g, step - 1 - g * OFFSET)
    for index in range(len(groups_of(0))):
        for end in range(2):
            combine(end, index)

    wait(tables.at[:, : (ring - 1) * 2 * count], table_send)
    for part in range(2):
        for direction in range(2):
            for hop in range(hops(direction, part)):
                wait(raw.at[0, :count], raw_send.at[part, direction, hop])
    for g in range(groups):
        wait(slabs.at[g, : slots - SLAB], slab_send.at[g])
        wait(slabs_raw.at[g, : (experts - 1) * ring * per], slab_raw_send.at[g])
        for direction in range(2):
            for part in range(2):
                for hop in range(hops(direction, part)):
                    wait(token_part(g, part, 0), token_send.at[g, part, direction, hop])
            for hop in range(hops(direction, g)):
                wait(hidden_own.at[g], hidden_send.at[g, direction, hop])
        wait(columns.at[g, : ring - 1], columns_send.at[g])
    for stream in range(2):
        for index in range(len(groups_of(stream))):
            wait(spread.at[0, : slots - SLAB], final_send.at[stream, index])

        @pl.when(jnp.logical_not(last(stream)))
        def _(stream=stream):
            for index in range(len(groups_of(stream))):
                wait(spread.at[0, :SLAB], final_send_same.at[stream, index])
            wait(residual.at[stream], residual_send.at[stream])
            wait(notes.at[stream], notes_send.at[stream])


def body(
    sections,
    act_down,
    act_up,
    norm_gain,
    gate_weight,
    up_weight,
    down_weight,
    routes_down,
    gates_down,
    routes_up,
    gates_up,
):
    count, depth = act_down.shape[1:]
    units = gate_weight.shape[1]
    hidden_units, piece = down_weight.shape[1:]
    ring = depth // piece
    per = SLAB // FOLD
    groups = 2 * CAP // per
    mine = -(-CAP // per)
    rows, slots, width = EXPERTS * per, EXPERTS * SLAB, depth // FOLD
    half = ring // 2
    dma = pltpu.SemaphoreType.DMA
    vmem = pl.BlockSpec(memory_space=pltpu.VMEM)
    anywhere = pl.BlockSpec(memory_space=pl.ANY)
    outs = pl.pallas_call(
        functools.partial(kernel, EXPERTS, sections),
        out_shape=[jax.ShapeDtypeStruct((count, depth), BF16)] * 2,
        in_specs=[vmem] * 7 + [anywhere] * 3,
        out_specs=[vmem] * 2,
        scratch_shapes=[
            pltpu.VMEM((2 * units, depth), BF16),
            pltpu.VMEM((piece, hidden_units), BF16),
            pltpu.VMEM((2, count, depth), BF16),
            pltpu.VMEM((ring, 2 * count, width), BF16),
            pltpu.VMEM((8, 2 * count), F32),
            pltpu.VMEM((8, ring * 2 * count), F32),
            pltpu.VMEM((groups, ring * rows, width), BF16),
            pltpu.VMEM((groups, ring * rows, width), BF16),
            pltpu.VMEM((groups, slots, width), BF16),
            pltpu.VMEM((groups, slots, width), BF16),
            pltpu.VMEM((groups, ring, (FOLD - 1) * rows, width), BF16),
            pltpu.VMEM((groups, ring * rows, units), BF16),
            pltpu.VMEM((groups, ring * rows, hidden_units), BF16),
            pltpu.VMEM((groups, ring, rows // 2, 2 * piece), BF16),
            pltpu.VMEM((groups, 2, ring // 2, rows // 2, 2 * piece), BF16),
            pltpu.VMEM((groups, slots, width), BF16),
            pltpu.VMEM((2, mine, slots, width), BF16),
            pltpu.VMEM((2, count, depth), BF16),
            pltpu.VMEM((2, count, 128), F32),
            pltpu.VMEM((2, count, 128), F32),
            pltpu.VMEM((2, count, depth), F32),
            dma((3,)),
            dma((2, 2, half)),
            dma((2, 2, half)),
            dma,
            dma,
            dma((groups,)),
            dma((groups,)),
            dma((groups,)),
            dma((groups,)),
            dma((groups, 2, 2, half)),
            dma((groups, 2, 2, half)),
            dma((groups, 2, half)),
            dma((groups, 2, half)),
            dma((groups,)),
            dma((groups,)),
            dma((groups,)),
            dma((2, mine)),
            dma((2, mine)),
            dma((2, mine)),
            dma((2,)),
            dma((2,)),
            dma((2,)),
            dma((2,)),
        ],
        compiler_params=pltpu.CompilerParams(
            collective_id=0, has_side_effects=True, vmem_limit_bytes=56 * 1024 * 1024
        ),
    )(
        act_down[0],
        act_up[0],
        norm_gain,
        routes_down[0].T,
        routes_up[0].T,
        gates_down[0].T,
        gates_up[0].T,
        gate_weight[0],
        up_weight[0],
        down_weight[0].T,
    )
    return tuple(out[None] for out in outs)


def solution(mesh):
    return jax.shard_map(
        functools.partial(body, mesh.shape["pipe"]),
        mesh=mesh,
        in_specs=(
            P("pipe", "expert", None),
            P("pipe", "expert", None),
            P("pipe", None),
            P("pipe", "expert", None),
            P("pipe", "expert", None),
            P("pipe", None, "expert"),
            P("pipe", "expert", None),
            P("pipe", "expert", None),
            P("pipe", "expert", None),
            P("pipe", "expert", None),
        ),
        out_specs=(P("pipe", "expert", None), P("pipe", "expert", None)),
        check_vma=False,
    )
```

```python
import functools

import jax
import jax.numpy as jnp
from jax import lax
from jax.experimental import pallas as pl
from jax.experimental.pallas import tpu as pltpu
from jax.sharding import PartitionSpec as P

EXPERTS = 8
CAP = 10
SLAB = 16
FOLD = 4
OFFSET = 1
EPSILON = 1e-06

MESH = pl.DeviceIdType.MESH
F32 = jnp.float32
BF16 = jnp.bfloat16


def one_hot(condition):
    return jnp.where(condition, 1.0, 0.0).astype(BF16)


def iota(shape, dimension):
    return lax.broadcasted_iota(jnp.int32, shape, dimension)


def dot_t(a, b):
    return lax.dot_general(a, b, (((1,), (1,)), ((), ())), preferred_element_type=F32)


def kernel(
    experts,
    sections,
    x_down,
    x_up,
    gain,
    routes_down,
    routes_up,
    gates_down,
    gates_up,
    gate_w,
    up_w,
    down_w,
    out_down,
    out_up,
    gate_up,
    down,
    normed,
    raw,
    table,
    tables,
    slabs_raw,
    landed_raw,
    slabs,
    landed,
    tokens,
    hidden_own,
    hidden,
    columns,
    returned,
    leaving,
    final,
    residual,
    notes,
    notes_here,
    token_notes,
    weight_copy,
    raw_send,
    raw_recv,
    table_send,
    table_recv,
    slab_raw_send,
    slab_raw_recv,
    slab_send,
    slab_recv,
    token_send,
    token_recv,
    hidden_send,
    hidden_recv,
    hidden_copy,
    columns_send,
    columns_recv,
    final_send,
    final_send_same,
    final_recv,
    residual_send,
    residual_recv,
    notes_send,
    notes_recv,
):
    groups, ring = tokens.shape[:2]
    per = SLAB // FOLD
    rows = experts * per
    slots = experts * SLAB
    count, depth = x_down.shape
    width = depth // FOLD
    units = gate_w.shape[0]
    pipe = lax.axis_index("pipe")
    position = lax.axis_index("expert")
    y = position // ring
    z = position % ring
    x_refs = (x_down, x_up)
    routes = (routes_down, routes_up)
    gates = (gates_down, gates_up)
    outs = (out_down, out_up)

    def groups_of(stream):
        return range(stream * CAP // per, -(-(stream + 1) * CAP // per))

    def streams_of(g):
        return [stream for stream in range(2) if g in groups_of(stream)]

    def at_y(k):
        return (pipe, lax.rem(y + k, experts) * ring + z)

    def at_z(k):
        return (pipe, y * ring + lax.rem(z + k, ring))

    barrier = pltpu.get_barrier_semaphore()

    def greet(device):
        pl.semaphore_signal(barrier, inc=1, device_id=device, device_id_type=MESH)

    @pl.loop(1, experts)
    def _(k):
        greet(at_y(k))

    @pl.loop(1, ring)
    def _(k):
        greet(at_z(k))

    @pl.when(pipe > 0)
    def _():
        @pl.loop(0, ring)
        def _(k):
            greet((pipe - 1, y * ring + k))

    @pl.when(pipe < sections - 1)
    def _():
        @pl.loop(0, ring)
        def _(k):
            greet((pipe + 1, y * ring + k))

    neighbours = jnp.where(pipe > 0, 1, 0) + jnp.where(pipe < sections - 1, 1, 0)
    greeted = experts - 1 + ring - 1 + ring * neighbours

    weight_copies = (
        pltpu.make_async_copy(gate_w, gate_up.at[:units], weight_copy.at[0]),
        pltpu.make_async_copy(up_w, gate_up.at[units:], weight_copy.at[1]),
        pltpu.make_async_copy(down_w, down, weight_copy.at[2]),
    )
    for copy in weight_copies:
        copy.start()

    def wait(ref, sem):
        pltpu.make_async_copy(ref, ref, sem).wait()

    def remote(source, target, sent, received, device):
        return pltpu.make_async_remote_copy(
            src_ref=source,
            dst_ref=target,
            send_sem=sent,
            recv_sem=received,
            device_id=device,
            device_id_type=MESH,
        )

    def normalize(stream):
        x_ref = x_refs[stream]
        total = jnp.zeros((count, 1), F32)
        for c in range(FOLD):
            part = x_ref[:, c * width : (c + 1) * width].astype(F32)
            total = total + jnp.sum(part * part, axis=-1, keepdims=True)
        inverse = lax.rsqrt(total / depth + EPSILON)
        for c in range(FOLD):
            cut = slice(c * width, (c + 1) * width)
            part = x_ref[:, cut].astype(F32)
            scaled = (part * inverse * gain[:, cut].astype(F32)).astype(BF16)
            if c == 0:
                raw[z, stream * count : (stream + 1) * count] = scaled
            else:
                normed[stream, :, cut] = scaled

    def number(stream):
        named = one_hot(routes[stream][...] == iota((experts, count), 0))
        earlier = one_hot(iota((count, count), 0) < iota((count, count), 1))
        rank = jnp.dot(named, earlier, preferred_element_type=F32)
        slot = jnp.sum(named.astype(F32) * rank, axis=0, keepdims=True) + stream * CAP
        expert = routes[stream][...].astype(F32)
        row = iota((128, count), 0)
        note = jnp.where(row == 0, expert, jnp.where(row == 1, slot, gates[stream][...]))
        notes[stream] = jnp.transpose(note)
        return expert, slot

    def send_table(numbers):
        row = iota((8, 2 * count), 0)
        expert, slot = (jnp.concatenate(pair, axis=1) for pair in zip(*numbers))
        table[...] = jnp.where(row == 0, expert, slot)
        target = tables.at[:, pl.ds(pl.multiple_of(z * 2 * count, 2 * count), 2 * count)]
        pltpu.make_async_copy(table, target, table_recv).start()

        @pl.loop(1, ring)
        def _(k):
            remote(table, target, table_send, table_recv, at_z(k)).start()

    def slab(k):
        return pl.ds(pl.multiple_of(k * SLAB, SLAB), SLAB)

    def matches(g, place, expert, slot):
        inside = place % per + g * per
        return (expert == (place // SLAB).astype(F32)) & (slot == inside.astype(F32))

    def pack(g, numbers):
        place = iota((slots, count), 0)
        total = jnp.zeros((slots, width), F32)
        for stream in streams_of(g):
            chosen = matches(g, place, *numbers[stream])
            for c in range(1, FOLD):
                total = total + jnp.dot(
                    one_hot(chosen & (place // per % FOLD == c)),
                    normed[stream, :, c * width : (c + 1) * width],
                    preferred_element_type=F32,
                )
        slabs[g] = total.astype(BF16)

    def dispatch(g):
        pltpu.make_async_copy(
            slabs.at[g, slab(y)], landed.at[g, slab(y)], slab_recv.at[g]
        ).start()

        @pl.loop(1, experts)
        def _(k):
            remote(
                slabs.at[g, slab(lax.rem(y + k, experts))],
                landed.at[g, slab(y)],
                slab_send.at[g],
                slab_recv.at[g],
                at_y(k),
            ).start()

    def last(stream):
        return pipe == (sections - 1 if stream == 0 else 0)

    def onward(stream):
        return pipe + 1 if stream == 0 else pipe - 1

    def send_residual(stream):
        pairs = (
            (x_refs[stream], residual, residual_send, residual_recv),
            (notes.at[stream], notes_here, notes_send, notes_recv),
        )

        @pl.when(last(stream))
        def _():
            for source, target, _, sem in pairs:
                end = 1 - stream
                pltpu.make_async_copy(source, target.at[end], sem.at[end]).start()

        @pl.when(jnp.logical_not(last(stream)))
        def _():
            for source, target, sent, sem in pairs:
                remote(
                    source,
                    target.at[stream],
                    sent.at[stream],
                    sem.at[stream],
                    (onward(stream), position),
                ).start()

    def hops(direction, part):
        return ring // 2 if direction == part % 2 else ring - 1 - ring // 2

    def behind(direction, k):
        return lax.rem(z + (ring - k if direction == 0 else k), ring)

    def ahead(direction):
        return at_z(1 if direction == 0 else ring - 1)

    half = (FOLD - 1) * rows // 2

    def raw_ring(part, direction, hop):
        block = raw.at[behind(direction, hop), part * count : (part + 1) * count]
        return remote(
            block,
            block,
            raw_send.at[part, direction, hop],
            raw_recv.at[part, direction, hop],
            ahead(direction),
        )

    def raw_stage(part, stage):
        for direction in range(2):
            if 1 <= stage <= hops(direction, part):
                wait(
                    raw.at[behind(direction, stage), part * count : (part + 1) * count],
                    raw_recv.at[part, direction, stage - 1],
                )
            if stage < hops(direction, part):
                raw_ring(part, direction, stage).start()

    def dispatch_raw(g):
        if g == 0:
            wait(tables, table_recv)
        size, span = ring * rows, ring * 2 * count
        row, lane = iota((size, span), 0), iota((size, span), 1)
        inside = row % per + g * per
        chosen = tables[0:1, :] == (row // (ring * per)).astype(F32)
        chosen = chosen & (tables[1:2, :] == inside.astype(F32))
        chosen = chosen & (row // per % ring == lane // (2 * count))
        slabs_raw[g] = jnp.dot(
            one_hot(chosen), raw[...].reshape(span, width), preferred_element_type=F32
        ).astype(BF16)

        def part(k):
            return pl.ds(pl.multiple_of(k * ring * per, ring * per), ring * per)

        pltpu.make_async_copy(
            slabs_raw.at[g, part(y)], landed_raw.at[g, part(y)], slab_raw_recv.at[g]
        ).start()

        @pl.loop(1, experts)
        def _(k):
            remote(
                slabs_raw.at[g, part(lax.rem(y + k, experts))],
                landed_raw.at[g, part(y)],
                slab_raw_send.at[g],
                slab_raw_recv.at[g],
                at_y(k),
            ).start()

    def token_part(g, part, owner):
        return tokens.at[g, owner, part * half : (part + 1) * half]

    def token_ring(g, part, direction, hop):
        block = token_part(g, part, behind(direction, hop))
        return remote(
            block,
            block,
            token_send.at[g, part, direction, hop],
            token_recv.at[g, part, direction, hop],
            ahead(direction),
        )

    def token_stage(g, stage):
        for part in range(2):
            for direction in range(2):
                if 1 <= stage <= hops(direction, part):
                    wait(
                        token_part(g, part, behind(direction, stage)),
                        token_recv.at[g, part, direction, stage - 1],
                    )
                if stage < hops(direction, part):
                    token_ring(g, part, direction, stage).start()

    def compact(g):
        wait(landed.at[g], slab_recv.at[g])
        size = (FOLD - 1) * rows
        row, place = iota((size, slots), 0), iota((size, slots), 1)
        same = row // rows + 1 == place // per % FOLD
        same = same & (row % rows == place // SLAB * per + place % per)
        tokens[g, z] = jnp.dot(
            one_hot(same), landed[g], preferred_element_type=F32
        ).astype(BF16)

    def hide(g):
        wait(landed_raw.at[g], slab_raw_recv.at[g])
        size = ring * rows
        row, place = iota((size, size), 0), iota((size, size), 1)
        same = (row // rows == place // per % ring) & (row % per == place % per)
        same = same & (row // per % experts == place // (ring * per))
        part = jnp.dot(one_hot(same), landed_raw[g], preferred_element_type=F32)
        total = dot_t(part.astype(BF16), gate_up[:, :width])
        for c in range(1, FOLD):
            part = tokens[g, :, (c - 1) * rows : c * rows, :].reshape(size, width)
            total = total + dot_t(part, gate_up[:, c * width : (c + 1) * width])
        hidden_own[g] = (jax.nn.silu(total[:, :units]) * total[:, units:]).astype(BF16)

    def hidden_part(g, owner):
        return hidden.at[g, :, pl.ds(pl.multiple_of(owner * units, units), units)]

    def hidden_copy_own(g):
        return pltpu.make_async_copy(hidden_own.at[g], hidden_part(g, z), hidden_copy.at[g])

    def hidden_stage(g, stage):
        if stage == 0:
            hidden_copy_own(g).start()
        for direction in range(2):
            if 1 <= stage <= hops(direction, g):
                wait(
                    hidden_part(g, behind(direction, stage)),
                    hidden_recv.at[g, direction, stage - 1],
                )
            if stage < hops(direction, g):
                block = hidden_part(g, behind(direction, stage))
                remote(
                    hidden_own.at[g] if stage == 0 else block,
                    block,
                    hidden_send.at[g, direction, stage],
                    hidden_recv.at[g, direction, stage],
                    ahead(direction),
                ).start()

    def project(g):
        hidden_copy_own(g).wait()
        size, piece = ring * rows, ring * per // 2
        row, place = iota((size, size), 0), iota((size, size), 1)
        same = (place // rows == row // per % ring) & (place % per == row % per)
        same = same & (place // per % experts == row // (ring * per))
        result = dot_t(hidden[g], down[...]).astype(BF16)
        result = jnp.dot(one_hot(same), result, preferred_element_type=F32)
        for k in range(experts):
            first, second = (
                result[(2 * k + i) * piece : (2 * k + i + 1) * piece] for i in range(2)
            )
            columns[g, k] = jnp.concatenate([first, second], axis=1).astype(BF16)
        target = returned.at[g, y]
        pltpu.make_async_copy(columns.at[g, y], target, columns_recv.at[g]).start()

        @pl.loop(1, experts)
        def _(k):
            remote(
                columns.at[g, lax.rem(y + k, experts)],
                target,
                columns_send.at[g],
                columns_recv.at[g],
                at_y(k),
            ).start()

    def note_tokens():
        row = iota((128, 2 * count), 0)
        for b in range(ring):
            lanes = slice(b * 2 * count, (b + 1) * 2 * count)
            note = jnp.where(row == 0, tables[0:1, lanes], tables[1:2, lanes])
            token_notes[b] = jnp.transpose(note)

    def collect(stream):
        members = groups_of(stream)
        for g in members:
            if streams_of(g)[0] == stream:
                wait(returned.at[g], columns_recv.at[g])
        near = ring // 2
        span = near * per
        size = len(members) * experts * span
        parts = [returned[g].reshape(experts * span, 2 * down.shape[0]) for g in members]
        source = jnp.concatenate(parts, axis=0)
        row, place = iota((near * count, size), 0), iota((near * count, size), 1)
        slot_here = place // (experts * span) * per + place % per + members[0] * per
        expert_here = place // span % experts
        for i in range(2):
            note = token_notes[i * near : (i + 1) * near, stream * count : (stream + 1) * count]
            note = note.reshape(near * count, 128)
            same = (note[:, 0:1] == expert_here.astype(F32)) & (row // count == place // per % near)
            same = same & (note[:, 1:2] == slot_here.astype(F32))
            picked = jnp.dot(one_hot(same), source, preferred_element_type=F32)
            cut = down.shape[0]
            picked = picked[:, i * cut : (i + 1) * cut]
            for b in range(near):
                first, second = (
                    picked[(2 * b + k) * count // 2 : (2 * b + k + 1) * count // 2]
                    for k in range(2)
                )
                joined = jnp.concatenate([first, second], axis=1)
                leaving[stream, i * near + b] = joined.astype(BF16)

    def send_back(stream):
        @pl.when(last(stream))
        def _():
            end = 1 - stream
            target = final.at[end, z]
            pltpu.make_async_copy(leaving.at[stream, z], target, final_recv.at[end]).start()

            @pl.loop(1, ring)
            def _(k):
                remote(
                    leaving.at[stream, lax.rem(z + k, ring)],
                    target,
                    final_send.at[stream],
                    final_recv.at[end],
                    at_z(k),
                ).start()

        @pl.when(jnp.logical_not(last(stream)))
        def _():
            target = final.at[stream, z]
            remote(
                leaving.at[stream, z],
                target,
                final_send_same.at[stream],
                final_recv.at[stream],
                (onward(stream), position),
            ).start()

            @pl.loop(1, ring)
            def _(k):
                to = lax.rem(z + k, ring)
                remote(
                    leaving.at[stream, to],
                    target,
                    final_send.at[stream],
                    final_recv.at[stream],
                    (onward(stream), y * ring + to),
                ).start()

    def combine(end):
        wait(residual.at[end], residual_recv.at[end])
        wait(notes_here.at[end], notes_recv.at[end])
        wait(final.at[end], final_recv.at[end])
        piece, size = down.shape[0], count // 2
        for k in range(ring // 2):
            cut = slice(2 * k * piece, 2 * (k + 1) * piece)
            pair = [final[end, 2 * k + i].astype(F32) for i in range(2)]
            for i in range(2):
                mine = slice(i * size, (i + 1) * size)
                lanes = slice(i * piece, (i + 1) * piece)
                out = jnp.concatenate([part[:, lanes] for part in pair], axis=1)
                total = residual[end, mine, cut].astype(F32)
                total = total + notes_here[end, mine, 2:3] * out
                outs[end][mine, cut] = total.astype(BF16)

    for stream in range(2):
        normalize(stream)
    pl.semaphore_wait(barrier, greeted)
    for part in range(2):
        raw_stage(part, 0)
    numbers = [number(0)]
    pack(0, numbers)
    dispatch(0)
    numbers.append(number(1))
    send_table(numbers)
    pack(1, numbers)
    dispatch(1)

    stages = ring // 2
    final_step = 2 * stages + 1

    def action(g, step):
        if step == 0:
            compact(g)
        if step <= stages:
            token_stage(g, step)
        if step == stages:
            hide(g)
        if stages <= step <= 2 * stages:
            hidden_stage(g, step - stages)
        if step == 2 * stages:
            project(g)

    for step in range(1, (groups - 1) * OFFSET + final_step + 2):
        if step <= stages:
            for part in range(2):
                raw_stage(part, step)
        if step == stages:
            for g in range(groups):
                dispatch_raw(g)
        for g in range(groups):
            if 0 <= step - 1 - g * OFFSET <= final_step:
                action(g, step - 1 - g * OFFSET)
        if step == stages + groups - 1:
            note_tokens()
        for stream in range(2):
            if step - 1 - groups_of(stream)[-1] * OFFSET == final_step:
                collect(stream)
                send_back(stream)
        if step + 1 < groups:
            pack(step + 1, numbers)
            dispatch(step + 1)
        if step == groups - 1:
            for stream in range(2):
                send_residual(stream)
            for copy in weight_copies:
                copy.wait()
    for end in range(2):
        combine(end)

    wait(tables.at[:, : (ring - 1) * 2 * count], table_send)
    for part in range(2):
        for direction in range(2):
            for hop in range(hops(direction, part)):
                wait(raw.at[0, :count], raw_send.at[part, direction, hop])
    for g in range(groups):
        wait(slabs.at[g, : slots - SLAB], slab_send.at[g])
        wait(slabs_raw.at[g, : (experts - 1) * ring * per], slab_raw_send.at[g])
        for direction in range(2):
            for part in range(2):
                for hop in range(hops(direction, part)):
                    wait(token_part(g, part, 0), token_send.at[g, part, direction, hop])
            for hop in range(hops(direction, g)):
                wait(hidden_own.at[g], hidden_send.at[g, direction, hop])
        wait(columns.at[g, : experts - 1], columns_send.at[g])
    for stream in range(2):
        wait(leaving.at[stream, : ring - 1], final_send.at[stream])

        @pl.when(jnp.logical_not(last(stream)))
        def _(stream=stream):
            wait(leaving.at[stream, 0], final_send_same.at[stream])
            wait(residual.at[stream], residual_send.at[stream])
            wait(notes.at[stream], notes_send.at[stream])


def body(
    sections,
    act_down,
    act_up,
    norm_gain,
    gate_weight,
    up_weight,
    down_weight,
    routes_down,
    gates_down,
    routes_up,
    gates_up,
):
    count, depth = act_down.shape[1:]
    units = gate_weight.shape[1]
    hidden_units, piece = down_weight.shape[1:]
    ring = depth // piece
    per = SLAB // FOLD
    groups = 2 * CAP // per
    rows, slots, width = EXPERTS * per, EXPERTS * SLAB, depth // FOLD
    half = ring // 2
    dma = pltpu.SemaphoreType.DMA
    vmem = pl.BlockSpec(memory_space=pltpu.VMEM)
    anywhere = pl.BlockSpec(memory_space=pl.ANY)
    outs = pl.pallas_call(
        functools.partial(kernel, EXPERTS, sections),
        out_shape=[jax.ShapeDtypeStruct((count, depth), BF16)] * 2,
        in_specs=[vmem] * 7 + [anywhere] * 3,
        out_specs=[vmem] * 2,
        scratch_shapes=[
            pltpu.VMEM((2 * units, depth), BF16),
            pltpu.VMEM((piece, hidden_units), BF16),
            pltpu.VMEM((2, count, depth), BF16),
            pltpu.VMEM((ring, 2 * count, width), BF16),
            pltpu.VMEM((8, 2 * count), F32),
            pltpu.VMEM((8, ring * 2 * count), F32),
            pltpu.VMEM((groups, ring * rows, width), BF16),
            pltpu.VMEM((groups, ring * rows, width), BF16),
            pltpu.VMEM((groups, slots, width), BF16),
            pltpu.VMEM((groups, slots, width), BF16),
            pltpu.VMEM((groups, ring, (FOLD - 1) * rows, width), BF16),
            pltpu.VMEM((groups, ring * rows, units), BF16),
            pltpu.VMEM((groups, ring * rows, hidden_units), BF16),
            pltpu.VMEM((groups, EXPERTS, ring * per // 2, 2 * piece), BF16),
            pltpu.VMEM((groups, EXPERTS, ring * per // 2, 2 * piece), BF16),
            pltpu.VMEM((2, ring, count // 2, 2 * piece), BF16),
            pltpu.VMEM((2, ring, count // 2, 2 * piece), BF16),
            pltpu.VMEM((2, count, depth), BF16),
            pltpu.VMEM((2, count, 128), F32),
            pltpu.VMEM((2, count, 128), F32),
            pltpu.VMEM((ring, 2 * count, 128), F32),
            dma((3,)),
            dma((2, 2, half)),
            dma((2, 2, half)),
            dma,
            dma,
            dma((groups,)),
            dma((groups,)),
            dma((groups,)),
            dma((groups,)),
            dma((groups, 2, 2, half)),
            dma((groups, 2, 2, half)),
            dma((groups, 2, half)),
            dma((groups, 2, half)),
            dma((groups,)),
            dma((groups,)),
            dma((groups,)),
            dma((2,)),
            dma((2,)),
            dma((2,)),
            dma((2,)),
            dma((2,)),
            dma((2,)),
            dma((2,)),
        ],
        compiler_params=pltpu.CompilerParams(
            collective_id=0, has_side_effects=True, vmem_limit_bytes=56 * 1024 * 1024
        ),
    )(
        act_down[0],
        act_up[0],
        norm_gain,
        routes_down[0].T,
        routes_up[0].T,
        gates_down[0].T,
        gates_up[0].T,
        gate_weight[0],
        up_weight[0],
        down_weight[0].T,
    )
    return tuple(out[None] for out in outs)


def solution(mesh):
    return jax.shard_map(
        functools.partial(body, mesh.shape["pipe"]),
        mesh=mesh,
        in_specs=(
            P("pipe", "expert", None),
            P("pipe", "expert", None),
            P("pipe", None),
            P("pipe", "expert", None),
            P("pipe", "expert", None),
            P("pipe", None, "expert"),
            P("pipe", "expert", None),
            P("pipe", "expert", None),
            P("pipe", "expert", None),
            P("pipe", "expert", None),
        ),
        out_specs=(P("pipe", "expert", None), P("pipe", "expert", None)),
        check_vma=False,
    )
```

```python
import functools

import jax
import jax.numpy as jnp
from jax import lax
from jax.experimental import pallas as pl
from jax.experimental.pallas import tpu as pltpu
from jax.sharding import PartitionSpec as P

EXPERTS = 8
CAP = 10
SLAB = 16
FOLD = 4
OFFSET = 1
EPSILON = 1e-06

MESH = pl.DeviceIdType.MESH
F32 = jnp.float32
BF16 = jnp.bfloat16


def one_hot(condition):
    return jnp.where(condition, 1.0, 0.0).astype(BF16)


def iota(shape, dimension):
    return lax.broadcasted_iota(jnp.int32, shape, dimension)


def dot_t(a, b):
    return lax.dot_general(a, b, (((1,), (1,)), ((), ())), preferred_element_type=F32)


def kernel(
    experts,
    sections,
    x_down,
    x_up,
    gain,
    routes_down,
    routes_up,
    gates_down,
    gates_up,
    gate_w,
    up_w,
    down_w,
    out_down,
    out_up,
    gate_up,
    down,
    normed,
    raw,
    table,
    tables,
    slabs_raw,
    landed_raw,
    slabs,
    landed,
    tokens,
    hidden_own,
    hidden,
    columns,
    returned,
    leaving,
    final,
    residual,
    notes,
    notes_here,
    token_notes,
    weight_copy,
    raw_send,
    raw_recv,
    table_send,
    table_recv,
    slab_raw_send,
    slab_raw_recv,
    slab_send,
    slab_recv,
    token_send,
    token_recv,
    hidden_send,
    hidden_recv,
    hidden_copy,
    columns_send,
    columns_recv,
    final_send,
    final_send_same,
    final_recv,
    residual_send,
    residual_recv,
    notes_send,
    notes_recv,
):
    groups, ring = tokens.shape[:2]
    per = SLAB // FOLD
    rows = experts * per
    slots = experts * SLAB
    count, depth = x_down.shape
    width = depth // FOLD
    units = gate_w.shape[0]
    pipe = lax.axis_index("pipe")
    position = lax.axis_index("expert")
    y = position // ring
    z = position % ring
    x_refs = (x_down, x_up)
    routes = (routes_down, routes_up)
    gates = (gates_down, gates_up)
    outs = (out_down, out_up)

    def groups_of(stream):
        return range(stream * CAP // per, -(-(stream + 1) * CAP // per))

    def streams_of(g):
        return [stream for stream in range(2) if g in groups_of(stream)]

    def at_y(k):
        return (pipe, lax.rem(y + k, experts) * ring + z)

    def at_z(k):
        return (pipe, y * ring + lax.rem(z + k, ring))

    barrier = pltpu.get_barrier_semaphore()

    def greet(device):
        pl.semaphore_signal(barrier, inc=1, device_id=device, device_id_type=MESH)

    @pl.loop(1, experts)
    def _(k):
        greet(at_y(k))

    @pl.loop(1, ring)
    def _(k):
        greet(at_z(k))

    @pl.when(pipe > 0)
    def _():
        @pl.loop(0, ring)
        def _(k):
            greet((pipe - 1, y * ring + k))

    @pl.when(pipe < sections - 1)
    def _():
        @pl.loop(0, ring)
        def _(k):
            greet((pipe + 1, y * ring + k))

    neighbours = jnp.where(pipe > 0, 1, 0) + jnp.where(pipe < sections - 1, 1, 0)
    greeted = experts - 1 + ring - 1 + ring * neighbours

    weight_copies = (
        pltpu.make_async_copy(gate_w, gate_up.at[:units], weight_copy.at[0]),
        pltpu.make_async_copy(up_w, gate_up.at[units:], weight_copy.at[1]),
        pltpu.make_async_copy(down_w, down, weight_copy.at[2]),
    )
    for copy in weight_copies:
        copy.start()

    def wait(ref, sem):
        pltpu.make_async_copy(ref, ref, sem).wait()

    def remote(source, target, sent, received, device):
        return pltpu.make_async_remote_copy(
            src_ref=source,
            dst_ref=target,
            send_sem=sent,
            recv_sem=received,
            device_id=device,
            device_id_type=MESH,
        )

    def normalize(stream):
        x_ref = x_refs[stream]
        total = jnp.zeros((count, 1), F32)
        for c in range(FOLD):
            part = x_ref[:, c * width : (c + 1) * width].astype(F32)
            total = total + jnp.sum(part * part, axis=-1, keepdims=True)
        inverse = lax.rsqrt(total / depth + EPSILON)
        for c in range(FOLD):
            cut = slice(c * width, (c + 1) * width)
            part = x_ref[:, cut].astype(F32)
            scaled = (part * inverse * gain[:, cut].astype(F32)).astype(BF16)
            if c == 0:
                raw[z, stream * count : (stream + 1) * count] = scaled
            else:
                normed[stream, :, cut] = scaled

    def number(stream):
        named = one_hot(routes[stream][...] == iota((experts, count), 0))
        earlier = one_hot(iota((count, count), 0) < iota((count, count), 1))
        rank = jnp.dot(named, earlier, preferred_element_type=F32)
        slot = jnp.sum(named.astype(F32) * rank, axis=0, keepdims=True) + stream * CAP
        expert = routes[stream][...].astype(F32)
        row = iota((128, count), 0)
        note = jnp.where(row == 0, expert, jnp.where(row == 1, slot, gates[stream][...]))
        notes[stream] = jnp.transpose(note)
        return expert, slot

    def send_table(numbers):
        row = iota((8, 2 * count), 0)
        expert, slot = (jnp.concatenate(pair, axis=1) for pair in zip(*numbers))
        table[...] = jnp.where(row == 0, expert, slot)
        target = tables.at[:, pl.ds(pl.multiple_of(z * 2 * count, 2 * count), 2 * count)]
        pltpu.make_async_copy(table, target, table_recv).start()

        @pl.loop(1, ring)
        def _(k):
            remote(table, target, table_send, table_recv, at_z(k)).start()

    def slab(k):
        return pl.ds(pl.multiple_of(k * SLAB, SLAB), SLAB)

    def matches(g, place, expert, slot):
        inside = place % per + g * per
        return (expert == (place // SLAB).astype(F32)) & (slot == inside.astype(F32))

    def pack(g, numbers):
        place = iota((slots, count), 0)
        total = jnp.zeros((slots, width), F32)
        for stream in streams_of(g):
            chosen = matches(g, place, *numbers[stream])
            for c in range(1, FOLD):
                total = total + jnp.dot(
                    one_hot(chosen & (place // per % FOLD == c)),
                    normed[stream, :, c * width : (c + 1) * width],
                    preferred_element_type=F32,
                )
        slabs[g] = total.astype(BF16)

    def dispatch(g):
        pltpu.make_async_copy(
            slabs.at[g, slab(y)], landed.at[g, slab(y)], slab_recv.at[g]
        ).start()

        @pl.loop(1, experts)
        def _(k):
            remote(
                slabs.at[g, slab(lax.rem(y + k, experts))],
                landed.at[g, slab(y)],
                slab_send.at[g],
                slab_recv.at[g],
                at_y(k),
            ).start()

    def last(stream):
        return pipe == (sections - 1 if stream == 0 else 0)

    def onward(stream):
        return pipe + 1 if stream == 0 else pipe - 1

    def send_residual(stream):
        pairs = (
            (x_refs[stream], residual, residual_send, residual_recv),
            (notes.at[stream], notes_here, notes_send, notes_recv),
        )

        @pl.when(last(stream))
        def _():
            for source, target, _, sem in pairs:
                end = 1 - stream
                pltpu.make_async_copy(source, target.at[end], sem.at[end]).start()

        @pl.when(jnp.logical_not(last(stream)))
        def _():
            for source, target, sent, sem in pairs:
                remote(
                    source,
                    target.at[stream],
                    sent.at[stream],
                    sem.at[stream],
                    (onward(stream), position),
                ).start()

    def hops(direction, part):
        return ring // 2 if direction == part % 2 else ring - 1 - ring // 2

    def behind(direction, k):
        return lax.rem(z + (ring - k if direction == 0 else k), ring)

    def ahead(direction):
        return at_z(1 if direction == 0 else ring - 1)

    half = (FOLD - 1) * rows // 2

    def raw_ring(part, direction, hop):
        block = raw.at[behind(direction, hop), part * count : (part + 1) * count]
        return remote(
            block,
            block,
            raw_send.at[part, direction, hop],
            raw_recv.at[part, direction, hop],
            ahead(direction),
        )

    def raw_stage(part, stage):
        for direction in range(2):
            if 1 <= stage <= hops(direction, part):
                wait(
                    raw.at[behind(direction, stage), part * count : (part + 1) * count],
                    raw_recv.at[part, direction, stage - 1],
                )
            if stage < hops(direction, part):
                raw_ring(part, direction, stage).start()

    def dispatch_raw(g):
        if g == 0:
            wait(tables, table_recv)
        size, span = ring * rows, ring * 2 * count
        row, lane = iota((size, span), 0), iota((size, span), 1)
        inside = row % per + g * per
        chosen = tables[0:1, :] == (row // (ring * per)).astype(F32)
        chosen = chosen & (tables[1:2, :] == inside.astype(F32))
        chosen = chosen & (row // per % ring == lane // (2 * count))
        slabs_raw[g] = jnp.dot(
            one_hot(chosen), raw[...].reshape(span, width), preferred_element_type=F32
        ).astype(BF16)

        def part(k):
            return pl.ds(pl.multiple_of(k * ring * per, ring * per), ring * per)

        pltpu.make_async_copy(
            slabs_raw.at[g, part(y)], landed_raw.at[g, part(y)], slab_raw_recv.at[g]
        ).start()

        @pl.loop(1, experts)
        def _(k):
            remote(
                slabs_raw.at[g, part(lax.rem(y + k, experts))],
                landed_raw.at[g, part(y)],
                slab_raw_send.at[g],
                slab_raw_recv.at[g],
                at_y(k),
            ).start()

    def token_part(g, part, owner):
        return tokens.at[g, owner, part * half : (part + 1) * half]

    def token_ring(g, part, direction, hop):
        block = token_part(g, part, behind(direction, hop))
        return remote(
            block,
            block,
            token_send.at[g, part, direction, hop],
            token_recv.at[g, part, direction, hop],
            ahead(direction),
        )

    def token_stage(g, stage):
        for part in range(2):
            for direction in range(2):
                if 1 <= stage <= hops(direction, part):
                    wait(
                        token_part(g, part, behind(direction, stage)),
                        token_recv.at[g, part, direction, stage - 1],
                    )
                if stage < hops(direction, part):
                    token_ring(g, part, direction, stage).start()

    def compact(g):
        wait(landed.at[g], slab_recv.at[g])
        size = (FOLD - 1) * rows
        row, place = iota((size, slots), 0), iota((size, slots), 1)
        same = row // rows + 1 == place // per % FOLD
        same = same & (row % rows == place // SLAB * per + place % per)
        tokens[g, z] = jnp.dot(
            one_hot(same), landed[g], preferred_element_type=F32
        ).astype(BF16)

    def hide(g):
        size = ring * rows
        total = jnp.zeros((size, 2 * units), F32)
        for c in range(1, FOLD):
            part = tokens[g, :, (c - 1) * rows : c * rows, :].reshape(size, width)
            total = total + dot_t(part, gate_up[:, c * width : (c + 1) * width])
        wait(landed_raw.at[g], slab_raw_recv.at[g])
        row, place = iota((size, size), 0), iota((size, size), 1)
        same = (row // rows == place // per % ring) & (row % per == place % per)
        same = same & (row // per % experts == place // (ring * per))
        part = jnp.dot(one_hot(same), landed_raw[g], preferred_element_type=F32)
        total = total + dot_t(part.astype(BF16), gate_up[:, :width])
        hidden_own[g] = (jax.nn.silu(total[:, :units]) * total[:, units:]).astype(BF16)

    def hidden_part(g, owner):
        return hidden.at[g, :, pl.ds(pl.multiple_of(owner * units, units), units)]

    def hidden_copy_own(g):
        return pltpu.make_async_copy(hidden_own.at[g], hidden_part(g, z), hidden_copy.at[g])

    def hidden_stage(g, stage):
        if stage == 0:
            hidden_copy_own(g).start()
        for direction in range(2):
            if 1 <= stage <= hops(direction, g):
                wait(
                    hidden_part(g, behind(direction, stage)),
                    hidden_recv.at[g, direction, stage - 1],
                )
            if stage < hops(direction, g):
                block = hidden_part(g, behind(direction, stage))
                remote(
                    hidden_own.at[g] if stage == 0 else block,
                    block,
                    hidden_send.at[g, direction, stage],
                    hidden_recv.at[g, direction, stage],
                    ahead(direction),
                ).start()

    def project(g):
        hidden_copy_own(g).wait()
        size, piece = ring * rows, ring * per // 2
        row, place = iota((size, size), 0), iota((size, size), 1)
        same = (place // rows == row // per % ring) & (place % per == row % per)
        same = same & (place // per % experts == row // (ring * per))
        result = dot_t(hidden[g], down[...]).astype(BF16)
        result = jnp.dot(one_hot(same), result, preferred_element_type=F32)
        for k in range(experts):
            first, second = (
                result[(2 * k + i) * piece : (2 * k + i + 1) * piece] for i in range(2)
            )
            columns[g, k] = jnp.concatenate([first, second], axis=1).astype(BF16)
        target = returned.at[g, y]
        pltpu.make_async_copy(columns.at[g, y], target, columns_recv.at[g]).start()

        @pl.loop(1, experts)
        def _(k):
            remote(
                columns.at[g, lax.rem(y + k, experts)],
                target,
                columns_send.at[g],
                columns_recv.at[g],
                at_y(k),
            ).start()

    def note_tokens():
        row = iota((128, 2 * count), 0)
        for b in range(ring):
            lanes = slice(b * 2 * count, (b + 1) * 2 * count)
            note = jnp.where(row == 0, tables[0:1, lanes], tables[1:2, lanes])
            token_notes[b] = jnp.transpose(note)

    def collect(stream):
        members = groups_of(stream)
        for g in members:
            if streams_of(g)[0] == stream:
                wait(returned.at[g], columns_recv.at[g])
        near = ring // 2
        span = near * per
        size = len(members) * experts * span
        parts = [returned[g].reshape(experts * span, 2 * down.shape[0]) for g in members]
        source = jnp.concatenate(parts, axis=0)
        row, place = iota((near * count, size), 0), iota((near * count, size), 1)
        slot_here = place // (experts * span) * per + place % per + members[0] * per
        expert_here = place // span % experts
        for i in range(2):
            note = token_notes[i * near : (i + 1) * near, stream * count : (stream + 1) * count]
            note = note.reshape(near * count, 128)
            same = (note[:, 0:1] == expert_here.astype(F32)) & (row // count == place // per % near)
            same = same & (note[:, 1:2] == slot_here.astype(F32))
            picked = jnp.dot(one_hot(same), source, preferred_element_type=F32)
            cut = down.shape[0]
            picked = picked[:, i * cut : (i + 1) * cut]
            for b in range(near):
                first, second = (
                    picked[(2 * b + k) * count // 2 : (2 * b + k + 1) * count // 2]
                    for k in range(2)
                )
                joined = jnp.concatenate([first, second], axis=1)
                leaving[stream, i * near + b] = joined.astype(BF16)

    def send_back(stream):
        @pl.when(last(stream))
        def _():
            end = 1 - stream
            target = final.at[end, z]
            pltpu.make_async_copy(leaving.at[stream, z], target, final_recv.at[end]).start()

            @pl.loop(1, ring)
            def _(k):
                remote(
                    leaving.at[stream, lax.rem(z + k, ring)],
                    target,
                    final_send.at[stream],
                    final_recv.at[end],
                    at_z(k),
                ).start()

        @pl.when(jnp.logical_not(last(stream)))
        def _():
            target = final.at[stream, z]
            remote(
                leaving.at[stream, z],
                target,
                final_send_same.at[stream],
                final_recv.at[stream],
                (onward(stream), position),
            ).start()

            @pl.loop(1, ring)
            def _(k):
                to = lax.rem(z + k, ring)
                remote(
                    leaving.at[stream, to],
                    target,
                    final_send.at[stream],
                    final_recv.at[stream],
                    (onward(stream), y * ring + to),
                ).start()

    def combine(end):
        wait(residual.at[end], residual_recv.at[end])
        wait(notes_here.at[end], notes_recv.at[end])
        wait(final.at[end], final_recv.at[end])
        piece, size = down.shape[0], count // 2
        for k in range(ring // 2):
            cut = slice(2 * k * piece, 2 * (k + 1) * piece)
            pair = [final[end, 2 * k + i].astype(F32) for i in range(2)]
            for i in range(2):
                mine = slice(i * size, (i + 1) * size)
                lanes = slice(i * piece, (i + 1) * piece)
                out = jnp.concatenate([part[:, lanes] for part in pair], axis=1)
                total = residual[end, mine, cut].astype(F32)
                total = total + notes_here[end, mine, 2:3] * out
                outs[end][mine, cut] = total.astype(BF16)

    for stream in range(2):
        normalize(stream)
    pl.semaphore_wait(barrier, greeted)
    for part in range(2):
        raw_stage(part, 0)
    numbers = [number(0)]
    pack(0, numbers)
    dispatch(0)
    numbers.append(number(1))
    send_table(numbers)
    pack(1, numbers)
    dispatch(1)

    stages = ring // 2
    final_step = 2 * stages + 1

    def action(g, step):
        if step == 0:
            compact(g)
        if step <= stages:
            token_stage(g, step)
        if step == stages:
            hide(g)
        if stages <= step <= 2 * stages:
            hidden_stage(g, step - stages)
        if step == 2 * stages:
            project(g)

    for step in range(1, (groups - 1) * OFFSET + final_step + 2):
        if step <= stages:
            for part in range(2):
                raw_stage(part, step)
        if step == stages:
            for g in range(groups):
                dispatch_raw(g)
        for g in range(groups):
            if 0 <= step - 1 - g * OFFSET <= final_step:
                action(g, step - 1 - g * OFFSET)
        if step == stages + groups - 1:
            note_tokens()
        for stream in range(2):
            if step - 1 - groups_of(stream)[-1] * OFFSET == final_step:
                collect(stream)
                send_back(stream)
        if step + 1 < groups:
            pack(step + 1, numbers)
            dispatch(step + 1)
        if step == groups - 1:
            for stream in range(2):
                send_residual(stream)
            for copy in weight_copies:
                copy.wait()
    for end in range(2):
        combine(end)

    wait(tables.at[:, : (ring - 1) * 2 * count], table_send)
    for part in range(2):
        for direction in range(2):
            for hop in range(hops(direction, part)):
                wait(raw.at[0, :count], raw_send.at[part, direction, hop])
    for g in range(groups):
        wait(slabs.at[g, : slots - SLAB], slab_send.at[g])
        wait(slabs_raw.at[g, : (experts - 1) * ring * per], slab_raw_send.at[g])
        for direction in range(2):
            for part in range(2):
                for hop in range(hops(direction, part)):
                    wait(token_part(g, part, 0), token_send.at[g, part, direction, hop])
            for hop in range(hops(direction, g)):
                wait(hidden_own.at[g], hidden_send.at[g, direction, hop])
        wait(columns.at[g, : experts - 1], columns_send.at[g])
    for stream in range(2):
        wait(leaving.at[stream, : ring - 1], final_send.at[stream])

        @pl.when(jnp.logical_not(last(stream)))
        def _(stream=stream):
            wait(leaving.at[stream, 0], final_send_same.at[stream])
            wait(residual.at[stream], residual_send.at[stream])
            wait(notes.at[stream], notes_send.at[stream])


def body(
    sections,
    act_down,
    act_up,
    norm_gain,
    gate_weight,
    up_weight,
    down_weight,
    routes_down,
    gates_down,
    routes_up,
    gates_up,
):
    count, depth = act_down.shape[1:]
    units = gate_weight.shape[1]
    hidden_units, piece = down_weight.shape[1:]
    ring = depth // piece
    per = SLAB // FOLD
    groups = 2 * CAP // per
    rows, slots, width = EXPERTS * per, EXPERTS * SLAB, depth // FOLD
    half = ring // 2
    dma = pltpu.SemaphoreType.DMA
    vmem = pl.BlockSpec(memory_space=pltpu.VMEM)
    anywhere = pl.BlockSpec(memory_space=pl.ANY)
    outs = pl.pallas_call(
        functools.partial(kernel, EXPERTS, sections),
        out_shape=[jax.ShapeDtypeStruct((count, depth), BF16)] * 2,
        in_specs=[vmem] * 7 + [anywhere] * 3,
        out_specs=[vmem] * 2,
        scratch_shapes=[
            pltpu.VMEM((2 * units, depth), BF16),
            pltpu.VMEM((piece, hidden_units), BF16),
            pltpu.VMEM((2, count, depth), BF16),
            pltpu.VMEM((ring, 2 * count, width), BF16),
            pltpu.VMEM((8, 2 * count), F32),
            pltpu.VMEM((8, ring * 2 * count), F32),
            pltpu.VMEM((groups, ring * rows, width), BF16),
            pltpu.VMEM((groups, ring * rows, width), BF16),
            pltpu.VMEM((groups, slots, width), BF16),
            pltpu.VMEM((groups, slots, width), BF16),
            pltpu.VMEM((groups, ring, (FOLD - 1) * rows, width), BF16),
            pltpu.VMEM((groups, ring * rows, units), BF16),
            pltpu.VMEM((groups, ring * rows, hidden_units), BF16),
            pltpu.VMEM((groups, EXPERTS, ring * per // 2, 2 * piece), BF16),
            pltpu.VMEM((groups, EXPERTS, ring * per // 2, 2 * piece), BF16),
            pltpu.VMEM((2, ring, count // 2, 2 * piece), BF16),
            pltpu.VMEM((2, ring, count // 2, 2 * piece), BF16),
            pltpu.VMEM((2, count, depth), BF16),
            pltpu.VMEM((2, count, 128), F32),
            pltpu.VMEM((2, count, 128), F32),
            pltpu.VMEM((ring, 2 * count, 128), F32),
            dma((3,)),
            dma((2, 2, half)),
            dma((2, 2, half)),
            dma,
            dma,
            dma((groups,)),
            dma((groups,)),
            dma((groups,)),
            dma((groups,)),
            dma((groups, 2, 2, half)),
            dma((groups, 2, 2, half)),
            dma((groups, 2, half)),
            dma((groups, 2, half)),
            dma((groups,)),
            dma((groups,)),
            dma((groups,)),
            dma((2,)),
            dma((2,)),
            dma((2,)),
            dma((2,)),
            dma((2,)),
            dma((2,)),
            dma((2,)),
        ],
        compiler_params=pltpu.CompilerParams(
            collective_id=0, has_side_effects=True, vmem_limit_bytes=56 * 1024 * 1024
        ),
    )(
        act_down[0],
        act_up[0],
        norm_gain,
        routes_down[0].T,
        routes_up[0].T,
        gates_down[0].T,
        gates_up[0].T,
        gate_weight[0],
        up_weight[0],
        down_weight[0].T,
    )
    return tuple(out[None] for out in outs)


def solution(mesh):
    return jax.shard_map(
        functools.partial(body, mesh.shape["pipe"]),
        mesh=mesh,
        in_specs=(
            P("pipe", "expert", None),
            P("pipe", "expert", None),
            P("pipe", None),
            P("pipe", "expert", None),
            P("pipe", "expert", None),
            P("pipe", None, "expert"),
            P("pipe", "expert", None),
            P("pipe", "expert", None),
            P("pipe", "expert", None),
            P("pipe", "expert", None),
        ),
        out_specs=(P("pipe", "expert", None), P("pipe", "expert", None)),
        check_vma=False,
    )
```
